32 devices in a mesh: groups: 2 (over y), res: 4 (over z), blk: 2 (over x), ch: 2 (over core).
Axes of the slice: x: 2, y: 2, z: 4, core: 2. Of those that a mesh axis runs over, the one named last changes fastest.
Arguments:
- single: bfloat16 [16384, 384], P(('groups', 'res')), parts along dimension 0, may hold values from -6 to 6
- frames: float32 [12, 16384], P(None, ('groups', 'res')), parts along dimension 1
- teacher: float32 [12, 16384], P(None, ('groups', 'res')), parts along dimension 1
- res_mask: int32 [16384], P(('groups', 'res')), parts along dimension 0, may hold values 0 or 1
- chain_ids: int32 [16384], P(('groups', 'res')), parts along dimension 0, may hold values from 0 to 31, never falling along the last dimension, each value on 1 to 512 neighbouring positions
- block_pairs: int32 [16, 12, 2], P('groups'), parts along dimension 0, may hold values from 0 to 63, as said below
- w_left: bfloat16 [384, 128], replicated, may hold values from -0.3125 to 0.3125
- w_right: bfloat16 [384, 128], replicated, may hold values from -0.3125 to 0.3125
- w_value: bfloat16 [384, 128], replicated, may hold values from -0.3125 to 0.3125
- w_pair: bfloat16 [128, 128], P(None, 'ch'), may hold values from -0.5 to 0.5
- pair_bias: float32 [128], P('ch'), may hold values from -3 to 3
- gate_vec: float32 [128], P('ch'), may hold values from -1 to 1
- w_out: bfloat16 [128, 384], replicated, may hold values from -0.5 to 0.5
Outputs:
- updated: bfloat16 [16384, 384], P(('groups', 'res')), parts along dimension 0
- pair_fape: float32 [192], P(('groups', 'res', 'blk')), parts along dimension 0
The draws below stay inside these ranges and needn't reach their ends.
There are 2 independent parts, one for each index of `groups`. The reference program is written for one: setup_inputs(seed, part) draws one part's arguments, and reference() takes and returns one part's arrays. A program takes and returns all parts, laid end to end along the dimension named above; an argument that names none is the same for every part. Nothing has to cross between parts.
Inputs may be any that keep to these rules, and one draw needn't show every extreme that they name: block_pairs[o,p,0] lies in blocks (o // 2) * 16 to (o // 2 + 1) * 16 - 1. Among the 12 pairs of one owner at most 4 have their second block in one run of blocks k * 16 to (k+1) * 16 - 1, and in every draw each owner has exactly 4 in one such run.
All inputs are finite; a program needn't handle non-finite values. No bound on the sum of `res_mask` on one device may be relied on, other than what follows from the above.
Results may differ from the reference program's by a relative error of at most 0.0059.
Values may be sent and summed in bfloat16 or wider, within the bound.
A program may use at most 64 MiB of HBM per device.

```python
import math
import jax
import jax.numpy as jnp
import numpy as np
from jax import lax

D = 384
C = 128
DH = 128
BLOCK = 128
PAIR_DEV = 12
NRES = 8192
NLB = 16
NOWN = 8
N_RES = 4
N_BLK = 2


def make_frames(key, which):
    base_key = jax.random.fold_in(key, 11)
    quat_key, trans_key = jax.random.split(base_key, 2)
    base_quat = jax.random.normal(quat_key, (4, NRES), jnp.float32)
    base_trans = 12.0 * jax.random.normal(trans_key, (3, NRES), jnp.float32)
    noise_key = jax.random.fold_in(key, 100 + which)
    qn_key, tn_key = jax.random.split(noise_key, 2)
    quat_noise = 0.3 * jax.random.normal(qn_key, (4, NRES), jnp.float32)
    trans_noise = 1.5 * jax.random.normal(tn_key, (3, NRES), jnp.float32)
    quat = base_quat + quat_noise
    quat = quat / jnp.sqrt(jnp.sum(quat * quat, axis=0, keepdims=True) + 1e-06)
    qw, qx, qy, qz = (quat[0], quat[1], quat[2], quat[3])
    rot_rows = [1.0 - 2.0 * (qy * qy + qz * qz), 2.0 * (qx * qy - qw * qz), 2.0 * (qx * qz + qw * qy), 2.0 * (qx * qy + qw * qz), 1.0 - 2.0 * (qx * qx + qz * qz), 2.0 * (qy * qz - qw * qx), 2.0 * (qx * qz - qw * qy), 2.0 * (qy * qz + qw * qx), 1.0 - 2.0 * (qx * qx + qy * qy)]
    trans = base_trans + trans_noise
    return jnp.concatenate([jnp.stack(rot_rows, axis=0), trans], axis=0).astype(jnp.float32)


def draw_frames(key, part):
    return make_frames(key, 1)


def draw_teacher(key, part):
    return make_frames(key, 2)


def draw_block_pairs(key, part):
    perm_key, near_key, far_key = jax.random.split(jax.random.fold_in(key, 5), 3)
    owner_keys = jax.random.split(perm_key, NOWN)
    shard_perms = jax.vmap(lambda one_key: jax.random.permutation(one_key, N_RES))(owner_keys).astype(jnp.int32)
    repeats = PAIR_DEV // N_RES + 1
    shard_seq = jnp.concatenate([shard_perms[:, :1], jnp.tile(shard_perms, (1, repeats))], axis=1)[:, :PAIR_DEV]
    far_local = jax.random.randint(far_key, (NOWN, PAIR_DEV), 0, NLB, jnp.int32)
    near_local = jax.random.randint(near_key, (NOWN, PAIR_DEV), 0, NLB, jnp.int32)
    owner_shard = (jnp.arange(NOWN, dtype=jnp.int32) // N_BLK)[:, None]
    first_ids = owner_shard * NLB + near_local
    second_ids = shard_seq * NLB + far_local
    return jnp.stack([first_ids, second_ids], axis=-1).astype(jnp.int32)


def place_ends(values, stream_key, least, largest):
    shape = values.shape
    spot = [jax.random.randint(jax.random.fold_in(stream_key, axis), (), 0, shape[axis]) for axis in range(len(shape))]
    values = values.at[tuple(spot)].set(least)
    longest = shape.index(max(shape))
    spot[longest] = (spot[longest] + 1) % shape[longest]
    return values.at[tuple(spot)].set(largest)


def level_of(own_key, extent, cuts, least, largest):
    loudness, own = 1.0, jax.random.fold_in(own_key, 6)
    for axis_at, shards_of in cuts:
        heights = jnp.exp(jax.random.uniform(jax.random.fold_in(own, axis_at), (shards_of,), jnp.float32, least / len(cuts), largest / len(cuts)))
        loudness = loudness * jnp.repeat(heights, extent[axis_at] // shards_of).reshape([-1 if axis == axis_at else 1 for axis in range(len(extent))])
    return loudness


def split_up(number_of, total, most, slope):
    loads = [(1 << 20) // math.isqrt(rank ** slope) + 1 for rank in range(2, number_of + 1)]
    rest, holding = total - most - (number_of - 1), [1] * (number_of - 1)
    while rest > 0:
        candidates = [i for i in range(number_of - 1) if holding[i] < most]
        whole, remaining = sum([loads[i] for i in candidates]), rest
        for i in candidates:
            extra = min(most - holding[i], max(1, remaining * loads[i] // whole), rest)
            holding[i] = holding[i] + extra
            rest = rest - extra
    return np.array([most] + holding)


def ragged(own_key, count, total, bound, slope):
    if count == 2:
        one = jax.random.randint(own_key, (), max(1, total - bound), min(bound, total - 1) + 1)
        return jnp.stack([one, total - one])
    tallies = jnp.asarray(split_up(count, total, bound, slope), jnp.int32)
    couples = (count - 1) // 2
    donor, taker = tallies[1:1 + 2 * couples:2], tallies[2:2 + 2 * couples:2]
    slack = jnp.minimum(donor - 1, bound - taker)
    moved = jax.random.randint(jax.random.fold_in(own_key, 1), (couples,), 0, 1 << 20) % (slack + 1)
    tallies = tallies.at[1:1 + 2 * couples:2].set(donor - moved).at[2:2 + 2 * couples:2].set(taker + moved)
    return tallies[jax.random.permutation(jax.random.fold_in(own_key, 2), count)]


def bell_draw(key, dims, spread, reach, cuts=(), kind=jnp.bfloat16):
    values = spread * jax.random.normal(key, dims, jnp.float32)
    if cuts:
        values = values * level_of(key, dims, cuts, -0.22, 0.18)
    return jnp.clip(values, -reach, reach).astype(kind)


def setup_inputs(seed: int = 0, part: int = 0) -> dict:
    seeds = jax.random.split(jax.random.key(seed), 14)
    own_keys = jax.random.split(jax.random.fold_in(seeds[13], part), 14)
    single = bell_draw(own_keys[0], (NRES, D), 1.0, 6.0, ((0, 4),))
    frames = draw_frames(jax.random.fold_in(jax.random.fold_in(seeds[13], part), 71), part)
    teacher = draw_teacher(jax.random.fold_in(jax.random.fold_in(seeds[13], part), 71), part)
    res_mask = place_ends((jax.random.randint(own_keys[3], (NRES,), 0, 8) < 7).astype(jnp.int32), jax.random.fold_in(own_keys[3], 1), 0, 1)
    chain_ids = jnp.searchsorted(jnp.cumsum(ragged(own_keys[4], NRES // (2 * BLOCK), NRES, 4 * BLOCK, 1)), jnp.arange(NRES), side="right").astype(jnp.int32)
    block_pairs = draw_block_pairs(jax.random.fold_in(jax.random.fold_in(seeds[13], part), 71), part)
    w_left = bell_draw(seeds[6], (D, C), D ** -0.5, 0.3125)
    w_right = bell_draw(seeds[7], (D, C), D ** -0.5, 0.3125)
    w_value = bell_draw(seeds[8], (D, DH), D ** -0.5, 0.3125)
    w_pair = bell_draw(seeds[9], (C, C), C ** -0.5, 0.5, ((1, 2),))
    pair_bias = bell_draw(seeds[10], (C,), 0.5, 3.0, ((0, 2),), jnp.float32)
    gate_vec = bell_draw(seeds[11], (C,), (C // 4) ** -0.5, 1.0, ((0, 2),), jnp.float32)
    w_out = bell_draw(seeds[12], (DH, D), DH ** -0.5, 0.5)
    return {"single": single, "frames": frames, "teacher": teacher, "res_mask": res_mask, "chain_ids": chain_ids, "block_pairs": block_pairs, "w_left": w_left, "w_right": w_right, "w_value": w_value, "w_pair": w_pair, "pair_bias": pair_bias, "gate_vec": gate_vec, "w_out": w_out}


def tile_logit(near_left, far_right, w_pair, pair_bias, gate_vec):
    outer_prod = (near_left.astype(jnp.float32)[:, :, None] * far_right.astype(jnp.float32).T[None, :, :]).astype(jnp.bfloat16)
    pair_act = jnp.einsum('kc,akb->acb', w_pair.astype(jnp.float32), outer_prod.astype(jnp.float32), precision=lax.Precision.HIGHEST)
    pair_act = pair_act + pair_bias[None, :, None]
    return jnp.einsum('c,acb->ab', gate_vec, jnp.maximum(pair_act, 0.0), precision=lax.Precision.HIGHEST)

def local_coords(geo_near, geo_far, offset):
    coords = []
    for axis_k in range(3):
        summed = jnp.zeros(geo_near.shape[:-2] + (geo_near.shape[-1], geo_far.shape[-1]), jnp.float32)
        for axis_m in range(3):
            gap_vec = geo_far[..., offset + 9 + axis_m, None, :] - geo_near[..., offset + 9 + axis_m, :, None]
            summed = summed + geo_near[..., offset + 3 * axis_m + axis_k, :, None] * gap_vec
        coords.append(summed)
    return coords

def finish(logit, value_near, value_far, geo_near, geo_far):
    live = geo_near[..., 24, :, None] * geo_far[..., 24, None, :]
    live = live * (geo_near[..., 25, :, None] != geo_far[..., 25, None, :]).astype(jnp.float32)
    weight = jax.nn.sigmoid(logit) * live
    weight_low = weight.astype(jnp.bfloat16)
    scale = BLOCK ** (-0.5)
    to_second = jnp.einsum('ab,ac->bc', weight_low.astype(jnp.float32), value_near.astype(jnp.float32), precision=lax.Precision.HIGHEST)
    to_second = (to_second * scale).astype(jnp.bfloat16)
    to_first = jnp.einsum('ab,bc->ac', weight_low.astype(jnp.float32), value_far.astype(jnp.float32), precision=lax.Precision.HIGHEST)
    to_first = (to_first * scale).astype(jnp.bfloat16)
    pred_coords = local_coords(geo_near, geo_far, 0)
    true_coords = local_coords(geo_near, geo_far, 12)
    dist_sq = jnp.zeros_like(weight)
    for axis_k in range(3):
        dist_sq = dist_sq + (pred_coords[axis_k] - true_coords[axis_k]) ** 2
    clipped = jnp.minimum(jnp.sqrt(dist_sq + 0.0001), 10.0)
    fape_value = jnp.sum(weight * clipped) / (BLOCK * BLOCK)
    return (fape_value, to_first, to_second)

def reference(single, frames, teacher, res_mask, chain_ids, block_pairs, w_left, w_right, w_value, w_pair, pair_bias, gate_vec, w_out):
    left_feats = jnp.dot(single, w_left, preferred_element_type=jnp.float32).astype(jnp.bfloat16)
    right_feats = jnp.dot(single, w_right, preferred_element_type=jnp.float32).astype(jnp.bfloat16)
    value_feats = jnp.dot(single, w_value, preferred_element_type=jnp.float32).astype(jnp.bfloat16)
    block_total = single.shape[0] // BLOCK
    left_blocks = left_feats.reshape(block_total, BLOCK, -1)
    right_blocks = right_feats.reshape(block_total, BLOCK, -1)
    value_blocks = value_feats.reshape(block_total, BLOCK, -1)
    geometry = jnp.concatenate([frames, teacher, res_mask[None, :].astype(jnp.float32), chain_ids[None, :].astype(jnp.float32)], axis=0)
    geo_blocks = geometry.reshape(26, block_total, BLOCK).transpose(1, 0, 2)
    flat_pairs = block_pairs.reshape(-1, 2).astype(jnp.int32)

    def one_pair(pair_ids):
        first_id = pair_ids[0]
        second_id = pair_ids[1]
        logit = tile_logit(left_blocks[first_id], right_blocks[second_id], w_pair, pair_bias, gate_vec)
        return finish(logit, value_blocks[first_id], value_blocks[second_id], geo_blocks[first_id], geo_blocks[second_id])
    pair_fape, to_first, to_second = lax.map(one_pair, flat_pairs)
    delta = jnp.zeros((block_total, BLOCK, value_feats.shape[1]), jnp.float32)
    delta = delta.at[flat_pairs[:, 0]].add(to_first.astype(jnp.float32))
    delta = delta.at[flat_pairs[:, 1]].add(to_second.astype(jnp.float32))
    delta_low = delta.reshape(single.shape[0], -1).astype(jnp.bfloat16)
    updated = (single.astype(jnp.float32) + jnp.dot(delta_low, w_out, preferred_element_type=jnp.float32)).astype(jnp.bfloat16)
    return (updated, pair_fape)
```

```python
import functools
import jax
import jax.numpy as jnp
from jax import lax
from jax.experimental import pallas as pl
from jax.experimental.pallas import tpu as pltpu
from jax.sharding import PartitionSpec as P

BLOCK = 128
CHUNK = 8
MESH = pl.DeviceIdType.MESH


def pair_kernel(
    sizes,
    pairs_ref,
    single_ref,
    frames_ref,
    teacher_ref,
    mask_ref,
    chain_ref,
    w_left_ref,
    w_right_ref,
    w_value_ref,
    gate_in_ref,
    w_out_ref,
    updated_ref,
    fape_ref,
    left_ref,
    value_ref,
    right_ref,
    geo_ref,
    far_geo_ref,
    pack_ref,
    w_bcast_ref,
    floor_ref,
    gate_ref,
    send_tab,
    near_tab,
    valid_tab,
    pos_tab,
    send_ref,
    recv_ref,
    geo_send_ref,
    geo_recv_ref,
    rhs_ref,
    logit_ref,
    geo_t_ref,
    weight_ref,
    first_ref,
    back_send_ref,
    back_recv_ref,
    delta_ref,
    half_send_ref,
    half_recv_ref,
    cross_send_ref,
    cross_recv_ref,
    low_own_ref,
    low_other_ref,
    fape_own_ref,
    fape_other_ref,
    w_sems,
    row_send_sem,
    row_recv_sem,
    geo_send_sem,
    geo_recv_sem,
    back_send_sem,
    back_recv_sem,
    half_sems,
    cross_send_sem,
    cross_recv_sem,
    low_send_sem,
    low_recv_sem,
    fape_sems,
):
    res_count, blk_count, blocks, pair_dev, slots, chans, parts = sizes
    total = res_count * slots
    half = blocks // 2
    piece = half // parts
    res = lax.axis_index("res")
    blk = lax.axis_index("blk")
    core = lax.axis_index("ch")
    f32, bf16 = jnp.float32, jnp.bfloat16

    barrier = pltpu.get_barrier_semaphore()

    def greet(step, carry):
        pl.semaphore_signal(
            barrier,
            inc=1,
            device_id={"res": lax.rem(res + step, res_count)},
            device_id_type=MESH,
        )
        return carry

    lax.fori_loop(1, res_count, greet, 0)
    pl.semaphore_signal(barrier, inc=1, device_id={"ch": 1 - core}, device_id_type=MESH)
    for step in range(1, blk_count):
        pl.semaphore_signal(
            barrier,
            inc=1,
            device_id={"blk": lax.rem(blk + step, blk_count)},
            device_id_type=MESH,
        )

    pack_ref[0] = gate_in_ref[...]

    def lookup(owner, shard):
        base = owner * (pair_dev * 2)
        zero = jnp.int32(0)
        rank = zero
        found = [[zero, zero, zero, zero] for _ in range(slots)]
        for p in range(pair_dev):
            first = pairs_ref[base + 2 * p]
            second = pairs_ref[base + 2 * p + 1]
            hit = (second >= shard * blocks) & (second < (shard + 1) * blocks)
            for j in range(slots):
                match = hit & (rank == 2 * j + core)
                old = found[j]
                found[j] = [
                    jnp.where(match, jnp.clip(first - res * blocks, 0, blocks - 1), old[0]),
                    jnp.where(match, second - shard * blocks, old[1]),
                    jnp.where(match, 1, old[2]),
                    jnp.where(match, p, old[3]),
                ]
            rank = rank + jnp.where(hit, 1, 0)
        return found

    def fill_tables(d, carry):
        out = lookup(lax.rem(res + d, res_count) * blk_count + blk, res)
        own = lookup(res * blk_count + blk, lax.rem(res - d + res_count, res_count))
        for j in range(slots):
            send_tab[d * slots + j] = out[j][1]
            near_tab[d * slots + j] = own[j][0]
            valid_tab[d * slots + j] = own[j][2]
            pos_tab[d * slots + j] = own[j][3]
        return carry

    lax.fori_loop(0, res_count, fill_tables, 0)

    def features(n, carry):
        rows = single_ref[pl.ds(pl.multiple_of(n * BLOCK, BLOCK), BLOCK), :]
        left_ref[n] = jnp.dot(rows, w_left_ref[...], preferred_element_type=f32).astype(bf16)
        right_ref[n] = jnp.dot(rows, w_right_ref[...], preferred_element_type=f32).astype(bf16)
        value_ref[n] = jnp.dot(rows, w_value_ref[...], preferred_element_type=f32).astype(bf16)
        lanes = pl.ds(pl.multiple_of(n * BLOCK, BLOCK), BLOCK)
        frames = frames_ref[:, lanes]
        teacher = teacher_ref[:, lanes]
        mask = mask_ref[:, lanes].astype(f32)
        chain = chain_ref[:, lanes].astype(f32)
        geo_ref[n] = jnp.concatenate(
            [frames, teacher, mask, chain, jnp.zeros((6, BLOCK), f32)], axis=0
        )
        far_geo_ref[n] = jnp.concatenate([frames[9:12], teacher[9:12], mask, chain], axis=0)
        return carry

    lax.fori_loop(0, blocks, features, 0)

    pl.semaphore_wait(barrier, res_count + blk_count - 1)

    w_copy = pltpu.make_async_remote_copy(
        src_ref=pack_ref.at[0],
        dst_ref=pack_ref.at[1],
        send_sem=w_sems.at[0],
        recv_sem=w_sems.at[1],
        device_id={"ch": 1 - core},
        device_id_type=MESH,
    )
    w_copy.start()

    def row_copies(d):
        target = {"res": lax.rem(res + d, res_count)}
        return (
            pltpu.make_async_remote_copy(
                src_ref=send_ref.at[d],
                dst_ref=recv_ref.at[d],
                send_sem=row_send_sem.at[d],
                recv_sem=row_recv_sem.at[d],
                device_id=target,
                device_id_type=MESH,
            ),
            pltpu.make_async_remote_copy(
                src_ref=geo_send_ref.at[d],
                dst_ref=geo_recv_ref.at[d],
                send_sem=geo_send_sem.at[d],
                recv_sem=geo_recv_sem.at[d],
                device_id=target,
                device_id_type=MESH,
            ),
        )

    def assemble(d, rows_to, geo_to):
        for j in range(slots):
            n = send_tab[d * slots + j]
            rows_to[d, j, :, 0:BLOCK] = right_ref[n]
            rows_to[d, j, :, BLOCK : 2 * BLOCK] = value_ref[n]
            geo_to[d, j] = far_geo_ref[n]

    def send_rows(d, carry):
        assemble(d, send_ref, geo_send_ref)
        for copy in row_copies(d):
            copy.start()
        return carry

    lax.fori_loop(1, res_count, send_rows, 0)
    assemble(0, recv_ref, geo_recv_ref)

    w_copy.wait()
    for h in range(2):
        floor_ref[h * chans : (h + 1) * chans, :] = jnp.concatenate(
            [pack_ref[h, 1]] * 2, axis=1
        )
        gate_ref[h * chans : (h + 1) * chans, :] = jnp.concatenate(
            [pack_ref[h, 2]] * 2, axis=1
        )
        for c in range(chans):
            row = jnp.broadcast_to(pack_ref[h, 0, c : c + 1, :], (16, BLOCK)).astype(bf16)
            w_bcast_ref[h * chans + c] = jnp.concatenate([row, row], axis=1)
    offset = -jnp.sum(floor_ref[:, 0:BLOCK] * gate_ref[:, 0:BLOCK], axis=0, keepdims=True)
    rhs_ref[...] = jnp.zeros_like(rhs_ref)
    fape_own_ref[...] = jnp.zeros_like(fape_own_ref)
    lane_ids = lax.broadcasted_iota(jnp.int32, (8, BLOCK), 1)

    def back_copy(d):
        return pltpu.make_async_remote_copy(
            src_ref=back_send_ref.at[d],
            dst_ref=back_recv_ref.at[d],
            send_sem=back_send_sem.at[d],
            recv_sem=back_recv_sem.at[d],
            device_id={"res": lax.rem(res - d + res_count, res_count)},
            device_id_type=MESH,
        )

    def one_pair(d, j):
        slot = d * slots + j
        near = near_tab[slot]
        right_t = recv_ref[d, j, :, 0:BLOCK].astype(f32).T.astype(bf16)
        rhs_ref[0:BLOCK, 0:BLOCK] = right_t
        rhs_ref[BLOCK : 2 * BLOCK, BLOCK : 2 * BLOCK] = right_t
        left = left_ref[near]
        left = jnp.concatenate([left[0:64], left[64:128]], axis=1)

        def channels(i, acc):
            base = i * CHUNK
            tiles = []
            for q in range(CHUNK):
                w_row = w_bcast_ref[base + q]
                for g in range(4):
                    tiles.append(left[g * 16 : (g + 1) * 16] * w_row)
            act = jnp.dot(
                jnp.concatenate(tiles, axis=0), rhs_ref[...], preferred_element_type=f32
            )
            for q in range(CHUNK):
                floor = floor_ref[pl.ds(base + q, 1), :]
                gate = gate_ref[pl.ds(base + q, 1), :]
                acc = acc + jnp.maximum(act[q * 64 : (q + 1) * 64], floor) * gate
            return acc

        acc = lax.fori_loop(
            0, 2 * chans // CHUNK, channels, jnp.zeros((64, 2 * BLOCK), f32)
        )
        logit_ref[0:64] = acc[:, 0:BLOCK] + offset
        logit_ref[64:128] = acc[:, BLOCK : 2 * BLOCK] + offset
        geo_t_ref[...] = geo_ref[near].T
        valid = valid_tab[slot].astype(f32)
        far = geo_recv_ref[d, j]

        def geometry(i, fape):
            rows = pl.ds(pl.multiple_of(i * 32, 32), 32)
            geo = geo_t_ref[rows, :]
            gaps = [
                far[m : m + 1] - geo[:, 9 + m : 10 + m] for m in range(3)
            ]
            true_gaps = [
                far[3 + m : 4 + m] - geo[:, 21 + m : 22 + m] for m in range(3)
            ]
            dist_sq = jnp.full((32, BLOCK), 0.0001, f32)
            for k in range(3):
                pred = sum(geo[:, 3 * m + k : 3 * m + k + 1] * gaps[m] for m in range(3))
                true = sum(
                    geo[:, 12 + 3 * m + k : 13 + 3 * m + k] * true_gaps[m] for m in range(3)
                )
                dist_sq = dist_sq + (pred - true) ** 2
            clipped = jnp.minimum(jnp.sqrt(dist_sq), 10.0)
            live = geo[:, 24:25] * (far[6:7] * valid)
            live = jnp.where(geo[:, 25:26] != far[7:8], live, 0.0)
            weight = jax.nn.sigmoid(logit_ref[rows, :]) * live
            weight_ref[rows, :] = weight.astype(bf16)
            scored = weight * clipped
            return fape + scored[0:8] + scored[8:16] + scored[16:24] + scored[24:32]

        fape = lax.fori_loop(0, 4, geometry, jnp.zeros((8, BLOCK), f32))
        fape = jnp.sum(jnp.sum(fape, axis=0, keepdims=True), axis=1, keepdims=True)
        fape = fape * (1.0 / (BLOCK * BLOCK))
        fape_own_ref[...] += jnp.where(lane_ids == pos_tab[slot], fape, 0.0)
        weight = weight_ref[...]
        scale = BLOCK ** (-0.5)
        to_second = lax.dot_general(
            weight, value_ref[near], (((0,), (0,)), ((), ())), preferred_element_type=f32
        )
        back_send_ref[d, j] = (to_second * scale).astype(bf16)
        to_first = jnp.dot(
            weight, recv_ref[d, j, :, BLOCK : 2 * BLOCK], preferred_element_type=f32
        )
        first_ref[d, j] = (to_first * scale).astype(bf16)

    def shard_step(d, carry):
        @pl.when(d > 0)
        def _():
            for copy in row_copies(d):
                copy.wait()

        def pair_step(j, inner):
            one_pair(d, j)
            return inner

        lax.fori_loop(0, slots, pair_step, 0)

        @pl.when(d > 0)
        def _():
            back_copy(d).start()

        return carry

    lax.fori_loop(0, res_count, shard_step, 0)

    fape_copy = pltpu.make_async_remote_copy(
        src_ref=fape_own_ref,
        dst_ref=fape_other_ref,
        send_sem=fape_sems.at[0],
        recv_sem=fape_sems.at[1],
        device_id={"ch": 1 - core},
        device_id_type=MESH,
    )
    fape_copy.start()

    row_id = lax.broadcasted_iota(jnp.int32, (blocks * 16, total * 16), 0)
    col_id = lax.broadcasted_iota(jnp.int32, (blocks * 16, total * 16), 1)
    same_row = (row_id % 16) == (col_id % 16)
    row_block = row_id // 16
    col_slot = lax.broadcasted_iota(jnp.int32, (1, total * 16), 1) // 16

    def spread(table):
        chosen = jnp.zeros((1, total * 16), jnp.int32)
        for s in range(total):
            chosen = jnp.where(col_slot == s, table[s], chosen)
        return jnp.where(same_row & (row_block == chosen), 1.0, 0.0).astype(bf16)

    near_hot = spread(near_tab)
    send_hot = spread(send_tab)

    def wait_back(d, carry):
        back_copy(d).wait()
        return carry

    def near_part(g):
        tiles = first_ref[:, :, g * 16 : (g + 1) * 16, :].reshape(total * 16, BLOCK)
        return jnp.dot(near_hot, tiles, preferred_element_type=f32)

    for g in range(BLOCK // 16):
        delta_ref[:, g * 16 : (g + 1) * 16, :] = near_part(g).reshape(blocks, 16, BLOCK)

    lax.fori_loop(1, res_count, wait_back, 0)
    back_recv_ref[0] = back_send_ref[0]
    for g in range(BLOCK // 16):
        tiles = back_recv_ref[:, :, g * 16 : (g + 1) * 16, :].reshape(total * 16, BLOCK)
        part = jnp.dot(send_hot, tiles, preferred_element_type=f32)
        delta_ref[:, g * 16 : (g + 1) * 16, :] += part.reshape(blocks, 16, BLOCK)

    half_send_ref[...] = delta_ref[pl.ds((1 - core) * half, half)].astype(bf16)

    half_copy = pltpu.make_async_remote_copy(
        src_ref=half_send_ref,
        dst_ref=half_recv_ref,
        send_sem=half_sems.at[0],
        recv_sem=half_sems.at[1],
        device_id={"ch": 1 - core},
        device_id_type=MESH,
    )
    half_copy.start()
    half_copy.wait()

    def cross_copy(step, i):
        return pltpu.make_async_remote_copy(
            src_ref=cross_send_ref.at[i],
            dst_ref=cross_recv_ref.at[step, i],
            send_sem=cross_send_sem.at[step, i],
            recv_sem=cross_recv_sem.at[step, i],
            device_id={"blk": lax.rem(blk + step, blk_count)},
            device_id_type=MESH,
        )

    def low_copy(i):
        return pltpu.make_async_remote_copy(
            src_ref=low_own_ref.at[i],
            dst_ref=low_other_ref.at[i],
            send_sem=low_send_sem.at[i],
            recv_sem=low_recv_sem.at[i],
            device_id={"ch": 1 - core},
            device_id_type=MESH,
        )

    def cross_start(i, carry):
        own = delta_ref[pl.ds(core * half + i * piece, piece)]
        own = (own + half_recv_ref[pl.ds(i * piece, piece)].astype(f32)).astype(bf16)
        cross_send_ref[i] = own
        cross_recv_ref[0, i] = own
        for step in range(1, blk_count):
            cross_copy(step, i).start()
        return carry

    lax.fori_loop(0, parts, cross_start, 0)

    def write(low, first_block):
        rows = pl.ds(pl.multiple_of(first_block * BLOCK, BLOCK), piece * BLOCK)
        low = low.reshape(piece * BLOCK, BLOCK)
        grown = jnp.dot(low, w_out_ref[...], preferred_element_type=f32)
        updated_ref[rows, :] = (single_ref[rows, :].astype(f32) + grown).astype(bf16)

    def own_piece(i, carry):
        for step in range(1, blk_count):
            cross_copy(step, i).wait()
        terms = [
            cross_recv_ref[lax.rem(blk - x + blk_count, blk_count), i].astype(f32)
            for x in range(blk_count)
        ]
        low_own_ref[i] = sum(terms[1:], terms[0]).astype(bf16)
        low_copy(i).start()
        write(low_own_ref[i], core * half + i * piece)
        return carry

    lax.fori_loop(0, parts, own_piece, 0)

    fape_copy.wait()
    fape_ref[...] = fape_own_ref[...] + fape_other_ref[...]

    def other_piece(i, carry):
        low_copy(i).wait()
        write(low_other_ref[i], (1 - core) * half + i * piece)
        return carry

    lax.fori_loop(0, parts, other_piece, 0)


def shards(
    single,
    frames,
    teacher,
    res_mask,
    chain_ids,
    block_pairs,
    w_left,
    w_right,
    w_value,
    w_pair,
    pair_bias,
    gate_vec,
    w_out,
):
    res_count = lax.axis_size("res")
    blk_count = lax.axis_size("blk")
    core_count = lax.axis_size("ch")
    row_count, width = single.shape
    blocks = row_count // BLOCK
    pair_dev = block_pairs.shape[1]
    capacity = 1 + (pair_dev + res_count - 2) // res_count
    slots = -(-capacity // core_count)
    chans = w_pair.shape[1]
    parts = 4
    half = blocks // 2
    piece = half // parts
    f32, bf16 = jnp.float32, jnp.bfloat16
    packed = jnp.stack(
        [
            w_pair.T.astype(f32),
            jnp.broadcast_to(-pair_bias[:, None], (chans, BLOCK)),
            jnp.broadcast_to(gate_vec[:, None], (chans, BLOCK)),
        ]
    )
    vmem = pl.BlockSpec(memory_space=pltpu.VMEM)
    smem = pl.BlockSpec(memory_space=pltpu.SMEM)
    dma = pltpu.SemaphoreType.DMA
    total = res_count * slots
    sizes = (res_count, blk_count, blocks, pair_dev, slots, chans, parts)
    updated, fape = pl.pallas_call(
        functools.partial(pair_kernel, sizes),
        out_shape=(
            jax.ShapeDtypeStruct((row_count, width), bf16),
            jax.ShapeDtypeStruct((8, BLOCK), f32),
        ),
        in_specs=[smem] + [vmem] * 10,
        out_specs=(vmem, vmem),
        scratch_shapes=[
            pltpu.VMEM((blocks, BLOCK, BLOCK), bf16),
            pltpu.VMEM((blocks, BLOCK, BLOCK), bf16),
            pltpu.VMEM((blocks, BLOCK, BLOCK), bf16),
            pltpu.VMEM((blocks, 32, BLOCK), f32),
            pltpu.VMEM((blocks, 8, BLOCK), f32),
            pltpu.VMEM((2, 3, chans, BLOCK), f32),
            pltpu.VMEM((2 * chans, 16, 2 * BLOCK), bf16),
            pltpu.VMEM((2 * chans, 2 * BLOCK), f32),
            pltpu.VMEM((2 * chans, 2 * BLOCK), f32),
            pltpu.SMEM((total,), jnp.int32),
            pltpu.SMEM((total,), jnp.int32),
            pltpu.SMEM((total,), jnp.int32),
            pltpu.SMEM((total,), jnp.int32),
            pltpu.VMEM((res_count, slots, BLOCK, 2 * BLOCK), bf16),
            pltpu.VMEM((res_count, slots, BLOCK, 2 * BLOCK), bf16),
            pltpu.VMEM((res_count, slots, 8, BLOCK), f32),
            pltpu.VMEM((res_count, slots, 8, BLOCK), f32),
            pltpu.VMEM((2 * BLOCK, 2 * BLOCK), bf16),
            pltpu.VMEM((BLOCK, BLOCK), f32),
            pltpu.VMEM((BLOCK, 32), f32),
            pltpu.VMEM((BLOCK, BLOCK), bf16),
            pltpu.VMEM((res_count, slots, BLOCK, BLOCK), bf16),
            pltpu.VMEM((res_count, slots, BLOCK, BLOCK), bf16),
            pltpu.VMEM((res_count, slots, BLOCK, BLOCK), bf16),
            pltpu.VMEM((blocks, BLOCK, BLOCK), f32),
            pltpu.VMEM((half, BLOCK, BLOCK), bf16),
            pltpu.VMEM((half, BLOCK, BLOCK), bf16),
            pltpu.VMEM((parts, piece, BLOCK, BLOCK), bf16),
            pltpu.VMEM((blk_count, parts, piece, BLOCK, BLOCK), bf16),
            pltpu.VMEM((parts, piece, BLOCK, BLOCK), bf16),
            pltpu.VMEM((parts, piece, BLOCK, BLOCK), bf16),
            pltpu.VMEM((8, BLOCK), f32),
            pltpu.VMEM((8, BLOCK), f32),
            dma((2,)),
            dma((res_count,)),
            dma((res_count,)),
            dma((res_count,)),
            dma((res_count,)),
            dma((res_count,)),
            dma((res_count,)),
            dma((2,)),
            dma((blk_count, parts)),
            dma((blk_count, parts)),
            dma((parts,)),
            dma((parts,)),
            dma((2,)),
        ],
        compiler_params=pltpu.CompilerParams(
            collective_id=0, has_side_effects=True, vmem_limit_bytes=40 * 1024 * 1024
        ),
    )(
        block_pairs.reshape(-1),
        single,
        frames,
        teacher,
        res_mask[None, :],
        chain_ids[None, :],
        w_left,
        w_right,
        w_value,
        packed,
        w_out,
    )
    return (updated, fape[0, :pair_dev])


def solution(mesh):
    placed = (
        P(("groups", "res"), None),
        P(None, ("groups", "res")),
        P(None, ("groups", "res")),
        P(("groups", "res")),
        P(("groups", "res")),
        P("groups", None, None),
        P(),
        P(),
        P(),
        P(None, "ch"),
        P("ch"),
        P("ch"),
        P(),
    )
    return jax.shard_map(
        shards,
        mesh=mesh,
        in_specs=placed,
        out_specs=(P(("groups", "res"), None), P(("groups", "res", "blk"))),
        check_vma=False,
    )
```

```python
import functools
import jax
import jax.numpy as jnp
from jax import lax
from jax.experimental import pallas as pl
from jax.experimental.pallas import tpu as pltpu
from jax.sharding import PartitionSpec as P

BLOCK = 128
CHUNK = 8
MESH = pl.DeviceIdType.MESH


def pair_kernel(
    sizes,
    pairs_ref,
    single_ref,
    frames_ref,
    teacher_ref,
    mask_ref,
    chain_ref,
    w_left_ref,
    w_right_ref,
    w_value_ref,
    gate_in_ref,
    w_out_ref,
    updated_ref,
    fape_ref,
    left_ref,
    value_ref,
    right_ref,
    geo_ref,
    far_geo_ref,
    pack_ref,
    w_bcast_ref,
    floor_ref,
    gate_ref,
    send_tab,
    near_tab,
    valid_tab,
    pos_tab,
    send_ref,
    recv_ref,
    geo_send_ref,
    geo_recv_ref,
    rhs_ref,
    logit_ref,
    geo_t_ref,
    weight_ref,
    first_ref,
    back_send_ref,
    back_recv_ref,
    delta_ref,
    half_send_ref,
    half_recv_ref,
    cross_send_ref,
    cross_recv_ref,
    low_own_ref,
    low_other_ref,
    fape_own_ref,
    fape_other_ref,
    w_sems,
    row_send_sem,
    row_recv_sem,
    geo_send_sem,
    geo_recv_sem,
    back_send_sem,
    back_recv_sem,
    half_sems,
    cross_send_sem,
    cross_recv_sem,
    low_send_sem,
    low_recv_sem,
    fape_sems,
):
    res_count, blk_count, blocks, pair_dev, slots, chans, parts = sizes
    total = res_count * slots
    half = blocks // 2
    piece = half // parts
    res = lax.axis_index("res")
    blk = lax.axis_index("blk")
    core = lax.axis_index("ch")
    f32, bf16 = jnp.float32, jnp.bfloat16

    barrier = pltpu.get_barrier_semaphore()

    def greet(step, carry):
        pl.semaphore_signal(
            barrier,
            inc=1,
            device_id={"res": lax.rem(res + step, res_count)},
            device_id_type=MESH,
        )
        return carry

    lax.fori_loop(1, res_count, greet, 0)
    pl.semaphore_signal(barrier, inc=1, device_id={"ch": 1 - core}, device_id_type=MESH)
    for step in range(1, blk_count):
        pl.semaphore_signal(
            barrier,
            inc=1,
            device_id={"blk": lax.rem(blk + step, blk_count)},
            device_id_type=MESH,
        )

    pack_ref[0] = gate_in_ref[...]

    def lookup(owner, shard):
        base = owner * (pair_dev * 2)
        zero = jnp.int32(0)
        rank = zero
        found = [[zero, zero, zero, zero] for _ in range(slots)]
        for p in range(pair_dev):
            first = pairs_ref[base + 2 * p]
            second = pairs_ref[base + 2 * p + 1]
            hit = (second >= shard * blocks) & (second < (shard + 1) * blocks)
            for j in range(slots):
                match = hit & (rank == 2 * j + core)
                old = found[j]
                found[j] = [
                    jnp.where(match, jnp.clip(first - res * blocks, 0, blocks - 1), old[0]),
                    jnp.where(match, second - shard * blocks, old[1]),
                    jnp.where(match, 1, old[2]),
                    jnp.where(match, p, old[3]),
                ]
            rank = rank + jnp.where(hit, 1, 0)
        return found

    def fill_tables(d, carry):
        out = lookup(lax.rem(res + d, res_count) * blk_count + blk, res)
        own = lookup(res * blk_count + blk, lax.rem(res - d + res_count, res_count))
        for j in range(slots):
            send_tab[d * slots + j] = out[j][1]
            near_tab[d * slots + j] = own[j][0]
            valid_tab[d * slots + j] = own[j][2]
            pos_tab[d * slots + j] = own[j][3]
        return carry

    lax.fori_loop(0, res_count, fill_tables, 0)

    def features(n, carry):
        rows = single_ref[pl.ds(pl.multiple_of(n * BLOCK, BLOCK), BLOCK), :]
        left_ref[n] = jnp.dot(rows, w_left_ref[...], preferred_element_type=f32).astype(bf16)
        right_ref[n] = jnp.dot(rows, w_right_ref[...], preferred_element_type=f32).astype(bf16)
        value_ref[n] = jnp.dot(rows, w_value_ref[...], preferred_element_type=f32).astype(bf16)
        lanes = pl.ds(pl.multiple_of(n * BLOCK, BLOCK), BLOCK)
        frames = frames_ref[:, lanes]
        teacher = teacher_ref[:, lanes]
        mask = mask_ref[:, lanes].astype(f32)
        chain = chain_ref[:, lanes].astype(f32)
        geo_ref[n] = jnp.concatenate(
            [frames, teacher, mask, chain, jnp.zeros((6, BLOCK), f32)], axis=0
        )
        far_geo_ref[n] = jnp.concatenate([frames[9:12], teacher[9:12], mask, chain], axis=0)
        return carry

    lax.fori_loop(0, blocks, features, 0)

    pl.semaphore_wait(barrier, res_count + blk_count - 1)

    w_copy = pltpu.make_async_remote_copy(
        src_ref=pack_ref.at[0],
        dst_ref=pack_ref.at[1],
        send_sem=w_sems.at[0],
        recv_sem=w_sems.at[1],
        device_id={"ch": 1 - core},
        device_id_type=MESH,
    )
    w_copy.start()

    def row_copies(d):
        target = {"res": lax.rem(res + d, res_count)}
        return (
            pltpu.make_async_remote_copy(
                src_ref=send_ref.at[d],
                dst_ref=recv_ref.at[d],
                send_sem=row_send_sem.at[d],
                recv_sem=row_recv_sem.at[d],
                device_id=target,
                device_id_type=MESH,
            ),
            pltpu.make_async_remote_copy(
                src_ref=geo_send_ref.at[d],
                dst_ref=geo_recv_ref.at[d],
                send_sem=geo_send_sem.at[d],
                recv_sem=geo_recv_sem.at[d],
                device_id=target,
                device_id_type=MESH,
            ),
        )

    def assemble(d, rows_to, geo_to):
        for j in range(slots):
            n = send_tab[d * slots + j]
            rows_to[d, j, :, 0:BLOCK] = right_ref[n]
            rows_to[d, j, :, BLOCK : 2 * BLOCK] = value_ref[n]
            geo_to[d, j] = far_geo_ref[n]

    def send_rows(d, carry):
        assemble(d, send_ref, geo_send_ref)
        for copy in row_copies(d):
            copy.start()
        return carry

    lax.fori_loop(1, res_count, send_rows, 0)
    assemble(0, recv_ref, geo_recv_ref)

    w_copy.wait()
    for h in range(2):
        floor_ref[h * chans : (h + 1) * chans, :] = jnp.concatenate(
            [pack_ref[h, 1]] * 2, axis=1
        )
        gate_ref[h * chans : (h + 1) * chans, :] = jnp.concatenate(
            [pack_ref[h, 2]] * 2, axis=1
        )
        for c in range(chans):
            row = jnp.broadcast_to(pack_ref[h, 0, c : c + 1, :], (16, BLOCK)).astype(bf16)
            w_bcast_ref[h * chans + c] = jnp.concatenate([row, row], axis=1)
    offset = -jnp.sum(floor_ref[:, 0:BLOCK] * gate_ref[:, 0:BLOCK], axis=0, keepdims=True)
    rhs_ref[...] = jnp.zeros_like(rhs_ref)
    fape_own_ref[...] = jnp.zeros_like(fape_own_ref)
    lane_ids = lax.broadcasted_iota(jnp.int32, (8, BLOCK), 1)

    def back_copy(d):
        return pltpu.make_async_remote_copy(
            src_ref=back_send_ref.at[d],
            dst_ref=back_recv_ref.at[d],
            send_sem=back_send_sem.at[d],
            recv_sem=back_recv_sem.at[d],
            device_id={"res": lax.rem(res - d + res_count, res_count)},
            device_id_type=MESH,
        )

    def one_pair(d, j):
        slot = d * slots + j
        near = near_tab[slot]
        right_t = recv_ref[d, j, :, 0:BLOCK].astype(f32).T.astype(bf16)
        rhs_ref[0:BLOCK, 0:BLOCK] = right_t
        rhs_ref[BLOCK : 2 * BLOCK, BLOCK : 2 * BLOCK] = right_t
        left = left_ref[near]
        left = jnp.concatenate([left[0:64], left[64:128]], axis=1)

        def channels(i, acc):
            base = i * CHUNK
            tiles = []
            for q in range(CHUNK):
                w_row = w_bcast_ref[base + q]
                for g in range(4):
                    tiles.append(left[g * 16 : (g + 1) * 16] * w_row)
            act = jnp.dot(
                jnp.concatenate(tiles, axis=0), rhs_ref[...], preferred_element_type=f32
            )
            for q in range(CHUNK):
                floor = floor_ref[pl.ds(base + q, 1), :]
                gate = gate_ref[pl.ds(base + q, 1), :]
                acc = acc + jnp.maximum(act[q * 64 : (q + 1) * 64], floor) * gate
            return acc

        acc = lax.fori_loop(
            0, 2 * chans // CHUNK, channels, jnp.zeros((64, 2 * BLOCK), f32), unroll=4
        )
        logit_ref[0:64] = acc[:, 0:BLOCK] + offset
        logit_ref[64:128] = acc[:, BLOCK : 2 * BLOCK] + offset
        geo_t_ref[...] = geo_ref[near].T
        valid = valid_tab[slot].astype(f32)
        far = geo_recv_ref[d, j]

        def geometry(i, fape):
            rows = pl.ds(pl.multiple_of(i * 32, 32), 32)
            geo = geo_t_ref[rows, :]
            gaps = [
                far[m : m + 1] - geo[:, 9 + m : 10 + m] for m in range(3)
            ]
            true_gaps = [
                far[3 + m : 4 + m] - geo[:, 21 + m : 22 + m] for m in range(3)
            ]
            dist_sq = jnp.full((32, BLOCK), 0.0001, f32)
            for k in range(3):
                pred = sum(geo[:, 3 * m + k : 3 * m + k + 1] * gaps[m] for m in range(3))
                true = sum(
                    geo[:, 12 + 3 * m + k : 13 + 3 * m + k] * true_gaps[m] for m in range(3)
                )
                dist_sq = dist_sq + (pred - true) ** 2
            clipped = jnp.minimum(jnp.sqrt(dist_sq), 10.0)
            live = geo[:, 24:25] * (far[6:7] * valid)
            live = jnp.where(geo[:, 25:26] != far[7:8], live, 0.0)
            weight = jax.nn.sigmoid(logit_ref[rows, :]) * live
            weight_ref[rows, :] = weight.astype(bf16)
            scored = weight * clipped
            return fape + scored[0:8] + scored[8:16] + scored[16:24] + scored[24:32]

        fape = lax.fori_loop(0, 4, geometry, jnp.zeros((8, BLOCK), f32))
        fape = jnp.sum(jnp.sum(fape, axis=0, keepdims=True), axis=1, keepdims=True)
        fape = fape * (1.0 / (BLOCK * BLOCK))
        fape_own_ref[...] += jnp.where(lane_ids == pos_tab[slot], fape, 0.0)
        weight = weight_ref[...]
        scale = BLOCK ** (-0.5)
        to_second = lax.dot_general(
            weight, value_ref[near], (((0,), (0,)), ((), ())), preferred_element_type=f32
        )
        back_send_ref[d, j] = (to_second * scale).astype(bf16)
        to_first = jnp.dot(
            weight, recv_ref[d, j, :, BLOCK : 2 * BLOCK], preferred_element_type=f32
        )
        first_ref[d, j] = (to_first * scale).astype(bf16)

    def shard_step(d, carry):
        @pl.when(d > 0)
        def _():
            for copy in row_copies(d):
                copy.wait()

        def pair_step(j, inner):
            one_pair(d, j)
            return inner

        lax.fori_loop(0, slots, pair_step, 0)

        @pl.when(d > 0)
        def _():
            back_copy(d).start()

        return carry

    lax.fori_loop(0, res_count, shard_step, 0)

    fape_copy = pltpu.make_async_remote_copy(
        src_ref=fape_own_ref,
        dst_ref=fape_other_ref,
        send_sem=fape_sems.at[0],
        recv_sem=fape_sems.at[1],
        device_id={"ch": 1 - core},
        device_id_type=MESH,
    )
    fape_copy.start()

    row_id = lax.broadcasted_iota(jnp.int32, (blocks * 16, total * 16), 0)
    col_id = lax.broadcasted_iota(jnp.int32, (blocks * 16, total * 16), 1)
    same_row = (row_id % 16) == (col_id % 16)
    row_block = row_id // 16
    col_slot = lax.broadcasted_iota(jnp.int32, (1, total * 16), 1) // 16

    def spread(table):
        chosen = jnp.zeros((1, total * 16), jnp.int32)
        for s in range(total):
            chosen = jnp.where(col_slot == s, table[s], chosen)
        return jnp.where(same_row & (row_block == chosen), 1.0, 0.0).astype(bf16)

    near_hot = spread(near_tab)
    send_hot = spread(send_tab)

    def wait_back(d, carry):
        back_copy(d).wait()
        return carry

    def near_part(g):
        tiles = first_ref[:, :, g * 16 : (g + 1) * 16, :].reshape(total * 16, BLOCK)
        return jnp.dot(near_hot, tiles, preferred_element_type=f32)

    for g in range(BLOCK // 16):
        delta_ref[:, g * 16 : (g + 1) * 16, :] = near_part(g).reshape(blocks, 16, BLOCK)

    lax.fori_loop(1, res_count, wait_back, 0)
    back_recv_ref[0] = back_send_ref[0]
    for g in range(BLOCK // 16):
        tiles = back_recv_ref[:, :, g * 16 : (g + 1) * 16, :].reshape(total * 16, BLOCK)
        part = jnp.dot(send_hot, tiles, preferred_element_type=f32)
        delta_ref[:, g * 16 : (g + 1) * 16, :] += part.reshape(blocks, 16, BLOCK)

    half_send_ref[...] = delta_ref[pl.ds((1 - core) * half, half)].astype(bf16)

    half_copy = pltpu.make_async_remote_copy(
        src_ref=half_send_ref,
        dst_ref=half_recv_ref,
        send_sem=half_sems.at[0],
        recv_sem=half_sems.at[1],
        device_id={"ch": 1 - core},
        device_id_type=MESH,
    )
    half_copy.start()
    half_copy.wait()

    def cross_copy(step, i):
        return pltpu.make_async_remote_copy(
            src_ref=cross_send_ref.at[i],
            dst_ref=cross_recv_ref.at[step, i],
            send_sem=cross_send_sem.at[step, i],
            recv_sem=cross_recv_sem.at[step, i],
            device_id={"blk": lax.rem(blk + step, blk_count)},
            device_id_type=MESH,
        )

    def low_copy(i):
        return pltpu.make_async_remote_copy(
            src_ref=low_own_ref.at[i],
            dst_ref=low_other_ref.at[i],
            send_sem=low_send_sem.at[i],
            recv_sem=low_recv_sem.at[i],
            device_id={"ch": 1 - core},
            device_id_type=MESH,
        )

    def cross_start(i, carry):
        own = delta_ref[pl.ds(core * half + i * piece, piece)]
        own = (own + half_recv_ref[pl.ds(i * piece, piece)].astype(f32)).astype(bf16)
        cross_send_ref[i] = own
        cross_recv_ref[0, i] = own
        for step in range(1, blk_count):
            cross_copy(step, i).start()
        return carry

    lax.fori_loop(0, parts, cross_start, 0)

    def write(low, first_block):
        rows = pl.ds(pl.multiple_of(first_block * BLOCK, BLOCK), piece * BLOCK)
        low = low.reshape(piece * BLOCK, BLOCK)
        grown = jnp.dot(low, w_out_ref[...], preferred_element_type=f32)
        updated_ref[rows, :] = (single_ref[rows, :].astype(f32) + grown).astype(bf16)

    def own_piece(i, carry):
        for step in range(1, blk_count):
            cross_copy(step, i).wait()
        terms = [
            cross_recv_ref[lax.rem(blk - x + blk_count, blk_count), i].astype(f32)
            for x in range(blk_count)
        ]
        low_own_ref[i] = sum(terms[1:], terms[0]).astype(bf16)
        low_copy(i).start()
        write(low_own_ref[i], core * half + i * piece)
        return carry

    lax.fori_loop(0, parts, own_piece, 0)

    fape_copy.wait()
    fape_ref[...] = fape_own_ref[...] + fape_other_ref[...]

    def other_piece(i, carry):
        low_copy(i).wait()
        write(low_other_ref[i], (1 - core) * half + i * piece)
        return carry

    lax.fori_loop(0, parts, other_piece, 0)


def shards(
    single,
    frames,
    teacher,
    res_mask,
    chain_ids,
    block_pairs,
    w_left,
    w_right,
    w_value,
    w_pair,
    pair_bias,
    gate_vec,
    w_out,
):
    res_count = lax.axis_size("res")
    blk_count = lax.axis_size("blk")
    core_count = lax.axis_size("ch")
    row_count, width = single.shape
    blocks = row_count // BLOCK
    pair_dev = block_pairs.shape[1]
    capacity = 1 + (pair_dev + res_count - 2) // res_count
    slots = -(-capacity // core_count)
    chans = w_pair.shape[1]
    parts = 4
    half = blocks // 2
    piece = half // parts
    f32, bf16 = jnp.float32, jnp.bfloat16
    packed = jnp.stack(
        [
            w_pair.T.astype(f32),
            jnp.broadcast_to(-pair_bias[:, None], (chans, BLOCK)),
            jnp.broadcast_to(gate_vec[:, None], (chans, BLOCK)),
        ]
    )
    vmem = pl.BlockSpec(memory_space=pltpu.VMEM)
    smem = pl.BlockSpec(memory_space=pltpu.SMEM)
    dma = pltpu.SemaphoreType.DMA
    total = res_count * slots
    sizes = (res_count, blk_count, blocks, pair_dev, slots, chans, parts)
    updated, fape = pl.pallas_call(
        functools.partial(pair_kernel, sizes),
        out_shape=(
            jax.ShapeDtypeStruct((row_count, width), bf16),
            jax.ShapeDtypeStruct((8, BLOCK), f32),
        ),
        in_specs=[smem] + [vmem] * 10,
        out_specs=(vmem, vmem),
        scratch_shapes=[
            pltpu.VMEM((blocks, BLOCK, BLOCK), bf16),
            pltpu.VMEM((blocks, BLOCK, BLOCK), bf16),
            pltpu.VMEM((blocks, BLOCK, BLOCK), bf16),
            pltpu.VMEM((blocks, 32, BLOCK), f32),
            pltpu.VMEM((blocks, 8, BLOCK), f32),
            pltpu.VMEM((2, 3, chans, BLOCK), f32),
            pltpu.VMEM((2 * chans, 16, 2 * BLOCK), bf16),
            pltpu.VMEM((2 * chans, 2 * BLOCK), f32),
            pltpu.VMEM((2 * chans, 2 * BLOCK), f32),
            pltpu.SMEM((total,), jnp.int32),
            pltpu.SMEM((total,), jnp.int32),
            pltpu.SMEM((total,), jnp.int32),
            pltpu.SMEM((total,), jnp.int32),
            pltpu.VMEM((res_count, slots, BLOCK, 2 * BLOCK), bf16),
            pltpu.VMEM((res_count, slots, BLOCK, 2 * BLOCK), bf16),
            pltpu.VMEM((res_count, slots, 8, BLOCK), f32),
            pltpu.VMEM((res_count, slots, 8, BLOCK), f32),
            pltpu.VMEM((2 * BLOCK, 2 * BLOCK), bf16),
            pltpu.VMEM((BLOCK, BLOCK), f32),
            pltpu.VMEM((BLOCK, 32), f32),
            pltpu.VMEM((BLOCK, BLOCK), bf16),
            pltpu.VMEM((res_count, slots, BLOCK, BLOCK), bf16),
            pltpu.VMEM((res_count, slots, BLOCK, BLOCK), bf16),
            pltpu.VMEM((res_count, slots, BLOCK, BLOCK), bf16),
            pltpu.VMEM((blocks, BLOCK, BLOCK), f32),
            pltpu.VMEM((half, BLOCK, BLOCK), bf16),
            pltpu.VMEM((half, BLOCK, BLOCK), bf16),
            pltpu.VMEM((parts, piece, BLOCK, BLOCK), bf16),
            pltpu.VMEM((blk_count, parts, piece, BLOCK, BLOCK), bf16),
            pltpu.VMEM((parts, piece, BLOCK, BLOCK), bf16),
            pltpu.VMEM((parts, piece, BLOCK, BLOCK), bf16),
            pltpu.VMEM((8, BLOCK), f32),
            pltpu.VMEM((8, BLOCK), f32),
            dma((2,)),
            dma((res_count,)),
            dma((res_count,)),
            dma((res_count,)),
            dma((res_count,)),
            dma((res_count,)),
            dma((res_count,)),
            dma((2,)),
            dma((blk_count, parts)),
            dma((blk_count, parts)),
            dma((parts,)),
            dma((parts,)),
            dma((2,)),
        ],
        compiler_params=pltpu.CompilerParams(
            collective_id=0, has_side_effects=True, vmem_limit_bytes=40 * 1024 * 1024
        ),
    )(
        block_pairs.reshape(-1),
        single,
        frames,
        teacher,
        res_mask[None, :],
        chain_ids[None, :],
        w_left,
        w_right,
        w_value,
        packed,
        w_out,
    )
    return (updated, fape[0, :pair_dev])


def solution(mesh):
    placed = (
        P(("groups", "res"), None),
        P(None, ("groups", "res")),
        P(None, ("groups", "res")),
        P(("groups", "res")),
        P(("groups", "res")),
        P("groups", None, None),
        P(),
        P(),
        P(),
        P(None, "ch"),
        P("ch"),
        P("ch"),
        P(),
    )
    return jax.shard_map(
        shards,
        mesh=mesh,
        in_specs=placed,
        out_specs=(P(("groups", "res"), None), P(("groups", "res", "blk"))),
        check_vma=False,
    )
```

```python
import functools
import jax
import jax.numpy as jnp
from jax import lax
from jax.experimental import pallas as pl
from jax.experimental.pallas import tpu as pltpu
from jax.sharding import PartitionSpec as P

BLOCK = 128
CHUNK = 8
MESH = pl.DeviceIdType.MESH


def pair_kernel(
    sizes,
    pairs_ref,
    single_ref,
    frames_ref,
    teacher_ref,
    mask_ref,
    chain_ref,
    w_left_ref,
    w_right_ref,
    w_value_ref,
    gate_in_ref,
    w_out_ref,
    updated_ref,
    fape_ref,
    left_ref,
    value_ref,
    right_ref,
    geo_ref,
    far_geo_ref,
    pack_ref,
    w_bcast_ref,
    floor_ref,
    gate_ref,
    send_tab,
    near_tab,
    valid_tab,
    pos_tab,
    send_ref,
    recv_ref,
    geo_send_ref,
    geo_recv_ref,
    rhs_ref,
    logit_ref,
    geo_t_ref,
    weight_ref,
    first_ref,
    back_send_ref,
    back_recv_ref,
    delta_ref,
    half_send_ref,
    half_recv_ref,
    cross_send_ref,
    cross_recv_ref,
    low_own_ref,
    low_other_ref,
    fape_own_ref,
    fape_other_ref,
    w_sems,
    row_send_sem,
    row_recv_sem,
    geo_send_sem,
    geo_recv_sem,
    back_send_sem,
    back_recv_sem,
    half_sems,
    cross_send_sem,
    cross_recv_sem,
    low_send_sem,
    low_recv_sem,
    fape_sems,
):
    res_count, blk_count, blocks, pair_dev, slots, chans, parts = sizes
    total = res_count * slots
    half = blocks // 2
    piece = half // parts
    res = lax.axis_index("res")
    blk = lax.axis_index("blk")
    core = lax.axis_index("ch")
    f32, bf16 = jnp.float32, jnp.bfloat16

    barrier = pltpu.get_barrier_semaphore()

    def greet(step, carry):
        pl.semaphore_signal(
            barrier,
            inc=1,
            device_id={"res": lax.rem(res + step, res_count)},
            device_id_type=MESH,
        )
        return carry

    lax.fori_loop(1, res_count, greet, 0)
    pl.semaphore_signal(barrier, inc=1, device_id={"ch": 1 - core}, device_id_type=MESH)
    for step in range(1, blk_count):
        pl.semaphore_signal(
            barrier,
            inc=1,
            device_id={"blk": lax.rem(blk + step, blk_count)},
            device_id_type=MESH,
        )

    pack_ref[0] = gate_in_ref[...]

    def lookup(owner, shard):
        base = owner * (pair_dev * 2)
        zero = jnp.int32(0)
        rank = zero
        found = [[zero, zero, zero, zero] for _ in range(slots)]
        for p in range(pair_dev):
            first = pairs_ref[base + 2 * p]
            second = pairs_ref[base + 2 * p + 1]
            hit = (second >= shard * blocks) & (second < (shard + 1) * blocks)
            for j in range(slots):
                match = hit & (rank == 2 * j + core)
                old = found[j]
                found[j] = [
                    jnp.where(match, jnp.clip(first - res * blocks, 0, blocks - 1), old[0]),
                    jnp.where(match, second - shard * blocks, old[1]),
                    jnp.where(match, 1, old[2]),
                    jnp.where(match, p, old[3]),
                ]
            rank = rank + jnp.where(hit, 1, 0)
        return found

    def fill_tables(d, carry):
        out = lookup(lax.rem(res + d, res_count) * blk_count + blk, res)
        own = lookup(res * blk_count + blk, lax.rem(res - d + res_count, res_count))
        for j in range(slots):
            send_tab[d * slots + j] = out[j][1]
            near_tab[d * slots + j] = own[j][0]
            valid_tab[d * slots + j] = own[j][2]
            pos_tab[d * slots + j] = own[j][3]
        return carry

    lax.fori_loop(0, res_count, fill_tables, 0)

    def features(n, carry):
        rows = single_ref[pl.ds(pl.multiple_of(n * BLOCK, BLOCK), BLOCK), :]
        left_ref[n] = jnp.dot(rows, w_left_ref[...], preferred_element_type=f32).astype(bf16)
        right_ref[n] = jnp.dot(rows, w_right_ref[...], preferred_element_type=f32).astype(bf16)
        value_ref[n] = jnp.dot(rows, w_value_ref[...], preferred_element_type=f32).astype(bf16)
        lanes = pl.ds(pl.multiple_of(n * BLOCK, BLOCK), BLOCK)
        frames = frames_ref[:, lanes]
        teacher = teacher_ref[:, lanes]
        mask = mask_ref[:, lanes].astype(f32)
        chain = chain_ref[:, lanes].astype(f32)
        geo_ref[n] = jnp.concatenate(
            [frames, teacher, mask, chain, jnp.zeros((6, BLOCK), f32)], axis=0
        )
        far_geo_ref[n] = jnp.concatenate([frames[9:12], teacher[9:12], mask, chain], axis=0)
        return carry

    lax.fori_loop(0, blocks, features, 0, unroll=4)

    pl.semaphore_wait(barrier, res_count + blk_count - 1)

    w_copy = pltpu.make_async_remote_copy(
        src_ref=pack_ref.at[0],
        dst_ref=pack_ref.at[1],
        send_sem=w_sems.at[0],
        recv_sem=w_sems.at[1],
        device_id={"ch": 1 - core},
        device_id_type=MESH,
    )
    w_copy.start()

    def row_copies(d):
        target = {"res": lax.rem(res + d, res_count)}
        return (
            pltpu.make_async_remote_copy(
                src_ref=send_ref.at[d],
                dst_ref=recv_ref.at[d],
                send_sem=row_send_sem.at[d],
                recv_sem=row_recv_sem.at[d],
                device_id=target,
                device_id_type=MESH,
            ),
            pltpu.make_async_remote_copy(
                src_ref=geo_send_ref.at[d],
                dst_ref=geo_recv_ref.at[d],
                send_sem=geo_send_sem.at[d],
                recv_sem=geo_recv_sem.at[d],
                device_id=target,
                device_id_type=MESH,
            ),
        )

    def assemble(d, rows_to, geo_to):
        for j in range(slots):
            n = send_tab[d * slots + j]
            rows_to[d, j, :, 0:BLOCK] = right_ref[n]
            rows_to[d, j, :, BLOCK : 2 * BLOCK] = value_ref[n]
            geo_to[d, j] = far_geo_ref[n]

    def send_rows(d, carry):
        assemble(d, send_ref, geo_send_ref)
        for copy in row_copies(d):
            copy.start()
        return carry

    lax.fori_loop(1, res_count, send_rows, 0)
    assemble(0, recv_ref, geo_recv_ref)

    w_copy.wait()
    for h in range(2):
        floor_ref[h * chans : (h + 1) * chans, :] = jnp.concatenate(
            [pack_ref[h, 1]] * 2, axis=1
        )
        gate_ref[h * chans : (h + 1) * chans, :] = jnp.concatenate(
            [pack_ref[h, 2]] * 2, axis=1
        )
        for c in range(chans):
            row = jnp.broadcast_to(pack_ref[h, 0, c : c + 1, :], (16, BLOCK)).astype(bf16)
            w_bcast_ref[h * chans + c] = jnp.concatenate([row, row], axis=1)
    offset = -jnp.sum(floor_ref[:, 0:BLOCK] * gate_ref[:, 0:BLOCK], axis=0, keepdims=True)
    rhs_ref[...] = jnp.zeros_like(rhs_ref)
    fape_own_ref[...] = jnp.zeros_like(fape_own_ref)
    lane_ids = lax.broadcasted_iota(jnp.int32, (8, BLOCK), 1)

    def back_copy(d):
        return pltpu.make_async_remote_copy(
            src_ref=back_send_ref.at[d],
            dst_ref=back_recv_ref.at[d],
            send_sem=back_send_sem.at[d],
            recv_sem=back_recv_sem.at[d],
            device_id={"res": lax.rem(res - d + res_count, res_count)},
            device_id_type=MESH,
        )

    def one_pair(d, j):
        slot = d * slots + j
        near = near_tab[slot]
        right_t = recv_ref[d, j, :, 0:BLOCK].astype(f32).T.astype(bf16)
        rhs_ref[0:BLOCK, 0:BLOCK] = right_t
        rhs_ref[BLOCK : 2 * BLOCK, BLOCK : 2 * BLOCK] = right_t
        left = left_ref[near]
        left = jnp.concatenate([left[0:64], left[64:128]], axis=1)

        def channels(i, acc):
            base = i * CHUNK
            tiles = []
            for q in range(CHUNK):
                w_row = w_bcast_ref[base + q]
                for g in range(4):
                    tiles.append(left[g * 16 : (g + 1) * 16] * w_row)
            act = jnp.dot(
                jnp.concatenate(tiles, axis=0), rhs_ref[...], preferred_element_type=f32
            )
            for q in range(CHUNK):
                floor = floor_ref[pl.ds(base + q, 1), :]
                gate = gate_ref[pl.ds(base + q, 1), :]
                acc = acc + jnp.maximum(act[q * 64 : (q + 1) * 64], floor) * gate
            return acc

        acc = lax.fori_loop(
            0, 2 * chans // CHUNK, channels, jnp.zeros((64, 2 * BLOCK), f32), unroll=2 * chans // CHUNK
        )
        logit_ref[0:64] = acc[:, 0:BLOCK] + offset
        logit_ref[64:128] = acc[:, BLOCK : 2 * BLOCK] + offset
        geo_t_ref[...] = geo_ref[near].T
        valid = valid_tab[slot].astype(f32)
        far = geo_recv_ref[d, j]

        def geometry(i, fape):
            rows = pl.ds(pl.multiple_of(i * 32, 32), 32)
            geo = geo_t_ref[rows, :]
            gaps = [
                far[m : m + 1] - geo[:, 9 + m : 10 + m] for m in range(3)
            ]
            true_gaps = [
                far[3 + m : 4 + m] - geo[:, 21 + m : 22 + m] for m in range(3)
            ]
            dist_sq = jnp.full((32, BLOCK), 0.0001, f32)
            for k in range(3):
                pred = sum(geo[:, 3 * m + k : 3 * m + k + 1] * gaps[m] for m in range(3))
                true = sum(
                    geo[:, 12 + 3 * m + k : 13 + 3 * m + k] * true_gaps[m] for m in range(3)
                )
                dist_sq = dist_sq + (pred - true) ** 2
            clipped = jnp.minimum(jnp.sqrt(dist_sq), 10.0)
            live = geo[:, 24:25] * (far[6:7] * valid)
            live = jnp.where(geo[:, 25:26] != far[7:8], live, 0.0)
            weight = jax.nn.sigmoid(logit_ref[rows, :]) * live
            weight_ref[rows, :] = weight.astype(bf16)
            scored = weight * clipped
            return fape + scored[0:8] + scored[8:16] + scored[16:24] + scored[24:32]

        fape = lax.fori_loop(0, 4, geometry, jnp.zeros((8, BLOCK), f32), unroll=2)
        fape = jnp.sum(jnp.sum(fape, axis=0, keepdims=True), axis=1, keepdims=True)
        fape = fape * (1.0 / (BLOCK * BLOCK))
        fape_own_ref[...] += jnp.where(lane_ids == pos_tab[slot], fape, 0.0)
        weight = weight_ref[...]
        scale = BLOCK ** (-0.5)
        to_second = lax.dot_general(
            weight, value_ref[near], (((0,), (0,)), ((), ())), preferred_element_type=f32
        )
        back_send_ref[d, j] = (to_second * scale).astype(bf16)
        to_first = jnp.dot(
            weight, recv_ref[d, j, :, BLOCK : 2 * BLOCK], preferred_element_type=f32
        )
        first_ref[d, j] = (to_first * scale).astype(bf16)

    def shard_step(d, carry):
        @pl.when(d > 0)
        def _():
            for copy in row_copies(d):
                copy.wait()

        def pair_step(j, inner):
            one_pair(d, j)
            return inner

        lax.fori_loop(0, slots, pair_step, 0)

        @pl.when(d > 0)
        def _():
            back_copy(d).start()

        return carry

    lax.fori_loop(0, res_count, shard_step, 0)

    fape_copy = pltpu.make_async_remote_copy(
        src_ref=fape_own_ref,
        dst_ref=fape_other_ref,
        send_sem=fape_sems.at[0],
        recv_sem=fape_sems.at[1],
        device_id={"ch": 1 - core},
        device_id_type=MESH,
    )
    fape_copy.start()

    row_id = lax.broadcasted_iota(jnp.int32, (blocks * 16, total * 16), 0)
    col_id = lax.broadcasted_iota(jnp.int32, (blocks * 16, total * 16), 1)
    same_row = (row_id % 16) == (col_id % 16)
    row_block = row_id // 16
    col_slot = lax.broadcasted_iota(jnp.int32, (1, total * 16), 1) // 16

    def spread(table):
        chosen = jnp.zeros((1, total * 16), jnp.int32)
        for s in range(total):
            chosen = jnp.where(col_slot == s, table[s], chosen)
        return jnp.where(same_row & (row_block == chosen), 1.0, 0.0).astype(bf16)

    near_hot = spread(near_tab)
    send_hot = spread(send_tab)

    def wait_back(d, carry):
        back_copy(d).wait()
        return carry

    def near_part(g):
        tiles = first_ref[:, :, g * 16 : (g + 1) * 16, :].reshape(total * 16, BLOCK)
        return jnp.dot(near_hot, tiles, preferred_element_type=f32)

    for g in range(BLOCK // 16):
        delta_ref[:, g * 16 : (g + 1) * 16, :] = near_part(g).reshape(blocks, 16, BLOCK)

    lax.fori_loop(1, res_count, wait_back, 0)
    back_recv_ref[0] = back_send_ref[0]
    for g in range(BLOCK // 16):
        tiles = back_recv_ref[:, :, g * 16 : (g + 1) * 16, :].reshape(total * 16, BLOCK)
        part = jnp.dot(send_hot, tiles, preferred_element_type=f32)
        delta_ref[:, g * 16 : (g + 1) * 16, :] += part.reshape(blocks, 16, BLOCK)

    half_send_ref[...] = delta_ref[pl.ds((1 - core) * half, half)].astype(bf16)

    half_copy = pltpu.make_async_remote_copy(
        src_ref=half_send_ref,
        dst_ref=half_recv_ref,
        send_sem=half_sems.at[0],
        recv_sem=half_sems.at[1],
        device_id={"ch": 1 - core},
        device_id_type=MESH,
    )
    half_copy.start()
    half_copy.wait()

    def cross_copy(step, i):
        return pltpu.make_async_remote_copy(
            src_ref=cross_send_ref.at[i],
            dst_ref=cross_recv_ref.at[step, i],
            send_sem=cross_send_sem.at[step, i],
            recv_sem=cross_recv_sem.at[step, i],
            device_id={"blk": lax.rem(blk + step, blk_count)},
            device_id_type=MESH,
        )

    def low_copy(i):
        return pltpu.make_async_remote_copy(
            src_ref=low_own_ref.at[i],
            dst_ref=low_other_ref.at[i],
            send_sem=low_send_sem.at[i],
            recv_sem=low_recv_sem.at[i],
            device_id={"ch": 1 - core},
            device_id_type=MESH,
        )

    def cross_start(i, carry):
        own = delta_ref[pl.ds(core * half + i * piece, piece)]
        own = (own + half_recv_ref[pl.ds(i * piece, piece)].astype(f32)).astype(bf16)
        cross_send_ref[i] = own
        cross_recv_ref[0, i] = own
        for step in range(1, blk_count):
            cross_copy(step, i).start()
        return carry

    lax.fori_loop(0, parts, cross_start, 0)

    def write(low, first_block):
        rows = pl.ds(pl.multiple_of(first_block * BLOCK, BLOCK), piece * BLOCK)
        low = low.reshape(piece * BLOCK, BLOCK)
        grown = jnp.dot(low, w_out_ref[...], preferred_element_type=f32)
        updated_ref[rows, :] = (single_ref[rows, :].astype(f32) + grown).astype(bf16)

    def own_piece(i, carry):
        for step in range(1, blk_count):
            cross_copy(step, i).wait()
        terms = [
            cross_recv_ref[lax.rem(blk - x + blk_count, blk_count), i].astype(f32)
            for x in range(blk_count)
        ]
        low_own_ref[i] = sum(terms[1:], terms[0]).astype(bf16)
        low_copy(i).start()
        write(low_own_ref[i], core * half + i * piece)
        return carry

    lax.fori_loop(0, parts, own_piece, 0)

    fape_copy.wait()
    fape_ref[...] = fape_own_ref[...] + fape_other_ref[...]

    def other_piece(i, carry):
        low_copy(i).wait()
        write(low_other_ref[i], (1 - core) * half + i * piece)
        return carry

    lax.fori_loop(0, parts, other_piece, 0)


def shards(
    single,
    frames,
    teacher,
    res_mask,
    chain_ids,
    block_pairs,
    w_left,
    w_right,
    w_value,
    w_pair,
    pair_bias,
    gate_vec,
    w_out,
):
    res_count = lax.axis_size("res")
    blk_count = lax.axis_size("blk")
    core_count = lax.axis_size("ch")
    row_count, width = single.shape
    blocks = row_count // BLOCK
    pair_dev = block_pairs.shape[1]
    capacity = 1 + (pair_dev + res_count - 2) // res_count
    slots = -(-capacity // core_count)
    chans = w_pair.shape[1]
    parts = 4
    half = blocks // 2
    piece = half // parts
    f32, bf16 = jnp.float32, jnp.bfloat16
    packed = jnp.stack(
        [
            w_pair.T.astype(f32),
            jnp.broadcast_to(-pair_bias[:, None], (chans, BLOCK)),
            jnp.broadcast_to(gate_vec[:, None], (chans, BLOCK)),
        ]
    )
    vmem = pl.BlockSpec(memory_space=pltpu.VMEM)
    smem = pl.BlockSpec(memory_space=pltpu.SMEM)
    dma = pltpu.SemaphoreType.DMA
    total = res_count * slots
    sizes = (res_count, blk_count, blocks, pair_dev, slots, chans, parts)
    updated, fape = pl.pallas_call(
        functools.partial(pair_kernel, sizes),
        out_shape=(
            jax.ShapeDtypeStruct((row_count, width), bf16),
            jax.ShapeDtypeStruct((8, BLOCK), f32),
        ),
        in_specs=[smem] + [vmem] * 10,
        out_specs=(vmem, vmem),
        scratch_shapes=[
            pltpu.VMEM((blocks, BLOCK, BLOCK), bf16),
            pltpu.VMEM((blocks, BLOCK, BLOCK), bf16),
            pltpu.VMEM((blocks, BLOCK, BLOCK), bf16),
            pltpu.VMEM((blocks, 32, BLOCK), f32),
            pltpu.VMEM((blocks, 8, BLOCK), f32),
            pltpu.VMEM((2, 3, chans, BLOCK), f32),
            pltpu.VMEM((2 * chans, 16, 2 * BLOCK), bf16),
            pltpu.VMEM((2 * chans, 2 * BLOCK), f32),
            pltpu.VMEM((2 * chans, 2 * BLOCK), f32),
            pltpu.SMEM((total,), jnp.int32),
            pltpu.SMEM((total,), jnp.int32),
            pltpu.SMEM((total,), jnp.int32),
            pltpu.SMEM((total,), jnp.int32),
            pltpu.VMEM((res_count, slots, BLOCK, 2 * BLOCK), bf16),
            pltpu.VMEM((res_count, slots, BLOCK, 2 * BLOCK), bf16),
            pltpu.VMEM((res_count, slots, 8, BLOCK), f32),
            pltpu.VMEM((res_count, slots, 8, BLOCK), f32),
            pltpu.VMEM((2 * BLOCK, 2 * BLOCK), bf16),
            pltpu.VMEM((BLOCK, BLOCK), f32),
            pltpu.VMEM((BLOCK, 32), f32),
            pltpu.VMEM((BLOCK, BLOCK), bf16),
            pltpu.VMEM((res_count, slots, BLOCK, BLOCK), bf16),
            pltpu.VMEM((res_count, slots, BLOCK, BLOCK), bf16),
            pltpu.VMEM((res_count, slots, BLOCK, BLOCK), bf16),
            pltpu.VMEM((blocks, BLOCK, BLOCK), f32),
            pltpu.VMEM((half, BLOCK, BLOCK), bf16),
            pltpu.VMEM((half, BLOCK, BLOCK), bf16),
            pltpu.VMEM((parts, piece, BLOCK, BLOCK), bf16),
            pltpu.VMEM((blk_count, parts, piece, BLOCK, BLOCK), bf16),
            pltpu.VMEM((parts, piece, BLOCK, BLOCK), bf16),
            pltpu.VMEM((parts, piece, BLOCK, BLOCK), bf16),
            pltpu.VMEM((8, BLOCK), f32),
            pltpu.VMEM((8, BLOCK), f32),
            dma((2,)),
            dma((res_count,)),
            dma((res_count,)),
            dma((res_count,)),
            dma((res_count,)),
            dma((res_count,)),
            dma((res_count,)),
            dma((2,)),
            dma((blk_count, parts)),
            dma((blk_count, parts)),
            dma((parts,)),
            dma((parts,)),
            dma((2,)),
        ],
        compiler_params=pltpu.CompilerParams(
            collective_id=0, has_side_effects=True, vmem_limit_bytes=40 * 1024 * 1024
        ),
    )(
        block_pairs.reshape(-1),
        single,
        frames,
        teacher,
        res_mask[None, :],
        chain_ids[None, :],
        w_left,
        w_right,
        w_value,
        packed,
        w_out,
    )
    return (updated, fape[0, :pair_dev])


def solution(mesh):
    placed = (
        P(("groups", "res"), None),
        P(None, ("groups", "res")),
        P(None, ("groups", "res")),
        P(("groups", "res")),
        P(("groups", "res")),
        P("groups", None, None),
        P(),
        P(),
        P(),
        P(None, "ch"),
        P("ch"),
        P("ch"),
        P(),
    )
    return jax.shard_map(
        shards,
        mesh=mesh,
        in_specs=placed,
        out_specs=(P(("groups", "res"), None), P(("groups", "res", "blk"))),
        check_vma=False,
    )
```

```python
import functools
import jax
import jax.numpy as jnp
from jax import lax
from jax.experimental import pallas as pl
from jax.experimental.pallas import tpu as pltpu
from jax.sharding import PartitionSpec as P

BLOCK = 128
CHUNK = 8
MESH = pl.DeviceIdType.MESH


def pair_kernel(
    sizes,
    pairs_ref,
    *refs,
):
    inputs, refs = refs[:12], refs[12:]
    (
        updated_ref,
        fape_ref,
        left_ref,
        value_ref,
        right_ref,
        geo_ref,
        far_geo_ref,
        pack_ref,
        w_bcast_ref,
        floor_ref,
        gate_ref,
        send_tab,
        near_tab,
        valid_tab,
        pos_tab,
        send_ref,
        recv_ref,
        geo_send_ref,
        geo_recv_ref,
        rhs_ref,
        logit_ref,
        geo_t_ref,
        weight_ref,
        first_ref,
        back_send_ref,
        back_recv_ref,
        delta_ref,
        half_send_ref,
        half_recv_ref,
        cross_send_ref,
        cross_recv_ref,
        low_own_ref,
        low_other_ref,
        fape_own_ref,
        fape_other_ref,
        w_sems,
        row_send_sem,
        row_recv_sem,
        geo_send_sem,
        geo_recv_sem,
        back_send_sem,
        back_recv_sem,
        half_sems,
        cross_send_sem,
        cross_recv_sem,
        low_send_sem,
        low_recv_sem,
        fape_sems,
        single_ref,
        frames_ref,
        teacher_ref,
        mask_ref,
        chain_ref,
        w_left_ref,
        w_right_ref,
        w_value_ref,
        w_pair_ref,
        bias_ref,
        gate_vec_ref,
        w_out_ref,
        load_sems,
    ) = refs
    held = (
        single_ref,
        frames_ref,
        teacher_ref,
        mask_ref,
        chain_ref,
        w_left_ref,
        w_right_ref,
        w_value_ref,
        w_pair_ref,
        bias_ref,
        gate_vec_ref,
        w_out_ref,
    )

    def load(i):
        return pltpu.make_async_copy(inputs[i], held[i], load_sems.at[i])

    for i in (1, 2, 3, 4, 0, 5, 6, 7, 8, 9, 10, 11):
        load(i).start()
    res_count, blk_count, blocks, pair_dev, slots, chans, parts = sizes
    total = res_count * slots
    half = blocks // 2
    piece = half // parts
    res = lax.axis_index("res")
    blk = lax.axis_index("blk")
    core = lax.axis_index("ch")
    f32, bf16 = jnp.float32, jnp.bfloat16

    barrier = pltpu.get_barrier_semaphore()

    def greet(step, carry):
        pl.semaphore_signal(
            barrier,
            inc=1,
            device_id={"res": lax.rem(res + step, res_count)},
            device_id_type=MESH,
        )
        return carry

    lax.fori_loop(1, res_count, greet, 0)
    pl.semaphore_signal(barrier, inc=1, device_id={"ch": 1 - core}, device_id_type=MESH)
    for step in range(1, blk_count):
        pl.semaphore_signal(
            barrier,
            inc=1,
            device_id={"blk": lax.rem(blk + step, blk_count)},
            device_id_type=MESH,
        )

    def lookup(owner, shard):
        base = owner * (pair_dev * 2)
        zero = jnp.int32(0)
        rank = zero
        found = [[zero, zero, zero, zero] for _ in range(slots)]
        for p in range(pair_dev):
            first = pairs_ref[base + 2 * p]
            second = pairs_ref[base + 2 * p + 1]
            hit = (second >= shard * blocks) & (second < (shard + 1) * blocks)
            for j in range(slots):
                match = hit & (rank == 2 * j + core)
                old = found[j]
                found[j] = [
                    jnp.where(match, jnp.clip(first - res * blocks, 0, blocks - 1), old[0]),
                    jnp.where(match, second - shard * blocks, old[1]),
                    jnp.where(match, 1, old[2]),
                    jnp.where(match, p, old[3]),
                ]
            rank = rank + jnp.where(hit, 1, 0)
        return found

    def fill_tables(d, carry):
        out = lookup(lax.rem(res + d, res_count) * blk_count + blk, res)
        own = lookup(res * blk_count + blk, lax.rem(res - d + res_count, res_count))
        for j in range(slots):
            send_tab[d * slots + j] = out[j][1]
            near_tab[d * slots + j] = own[j][0]
            valid_tab[d * slots + j] = own[j][2]
            pos_tab[d * slots + j] = own[j][3]
        return carry

    lax.fori_loop(0, res_count, fill_tables, 0)
    for i in range(12):
        load(i).wait()
    pack_ref[0, 0] = w_pair_ref[...].astype(f32)
    pack_ref[0, 1] = jnp.broadcast_to(-bias_ref[...], (BLOCK, chans)).T
    pack_ref[0, 2] = jnp.broadcast_to(gate_vec_ref[...], (BLOCK, chans)).T

    def features(n, carry):
        rows = single_ref[pl.ds(pl.multiple_of(n * BLOCK, BLOCK), BLOCK), :]
        left_ref[n] = jnp.dot(rows, w_left_ref[...], preferred_element_type=f32).astype(bf16)
        right_ref[n] = jnp.dot(rows, w_right_ref[...], preferred_element_type=f32).astype(bf16)
        value_ref[n] = jnp.dot(rows, w_value_ref[...], preferred_element_type=f32).astype(bf16)
        lanes = pl.ds(pl.multiple_of(n * BLOCK, BLOCK), BLOCK)
        frames = frames_ref[:, lanes]
        teacher = teacher_ref[:, lanes]
        mask = mask_ref[:, lanes].astype(f32)
        chain = chain_ref[:, lanes].astype(f32)
        geo_ref[n] = jnp.concatenate(
            [frames, teacher, mask, chain, jnp.zeros((6, BLOCK), f32)], axis=0
        )
        far_geo_ref[n] = jnp.concatenate([frames[9:12], teacher[9:12], mask, chain], axis=0)
        return carry

    lax.fori_loop(0, blocks, features, 0, unroll=4)

    pl.semaphore_wait(barrier, res_count + blk_count - 1)

    w_copy = pltpu.make_async_remote_copy(
        src_ref=pack_ref.at[0],
        dst_ref=pack_ref.at[1],
        send_sem=w_sems.at[0],
        recv_sem=w_sems.at[1],
        device_id={"ch": 1 - core},
        device_id_type=MESH,
    )
    w_copy.start()

    def row_copies(d):
        target = {"res": lax.rem(res + d, res_count)}
        return (
            pltpu.make_async_remote_copy(
                src_ref=send_ref.at[d],
                dst_ref=recv_ref.at[d],
                send_sem=row_send_sem.at[d],
                recv_sem=row_recv_sem.at[d],
                device_id=target,
                device_id_type=MESH,
            ),
            pltpu.make_async_remote_copy(
                src_ref=geo_send_ref.at[d],
                dst_ref=geo_recv_ref.at[d],
                send_sem=geo_send_sem.at[d],
                recv_sem=geo_recv_sem.at[d],
                device_id=target,
                device_id_type=MESH,
            ),
        )

    def assemble(d, rows_to, geo_to):
        for j in range(slots):
            n = send_tab[d * slots + j]
            rows_to[d, j, :, 0:BLOCK] = right_ref[n]
            rows_to[d, j, :, BLOCK : 2 * BLOCK] = value_ref[n]
            geo_to[d, j] = far_geo_ref[n]

    def send_rows(d, carry):
        assemble(d, send_ref, geo_send_ref)
        for copy in row_copies(d):
            copy.start()
        return carry

    lax.fori_loop(1, res_count, send_rows, 0)
    assemble(0, recv_ref, geo_recv_ref)

    w_copy.wait()
    for h in range(2):
        floor_ref[h * chans : (h + 1) * chans, :] = jnp.concatenate(
            [pack_ref[h, 1]] * 2, axis=1
        )
        gate_ref[h * chans : (h + 1) * chans, :] = jnp.concatenate(
            [pack_ref[h, 2]] * 2, axis=1
        )
        for c in range(chans):
            row = jnp.broadcast_to(pack_ref[h, 0, c : c + 1, :], (16, BLOCK)).astype(bf16)
            w_bcast_ref[h * chans + c] = jnp.concatenate([row, row], axis=1)
    offset = -jnp.sum(floor_ref[:, 0:BLOCK] * gate_ref[:, 0:BLOCK], axis=0, keepdims=True)
    rhs_ref[...] = jnp.zeros_like(rhs_ref)
    fape_own_ref[...] = jnp.zeros_like(fape_own_ref)
    lane_ids = lax.broadcasted_iota(jnp.int32, (8, BLOCK), 1)

    def back_copy(d):
        return pltpu.make_async_remote_copy(
            src_ref=back_send_ref.at[d],
            dst_ref=back_recv_ref.at[d],
            send_sem=back_send_sem.at[d],
            recv_sem=back_recv_sem.at[d],
            device_id={"res": lax.rem(res - d + res_count, res_count)},
            device_id_type=MESH,
        )

    def one_pair(d, j):
        slot = d * slots + j
        near = near_tab[slot]
        right_t = recv_ref[d, j, :, 0:BLOCK].astype(f32).T.astype(bf16)
        rhs_ref[0:BLOCK, 0:BLOCK] = right_t
        rhs_ref[BLOCK : 2 * BLOCK, BLOCK : 2 * BLOCK] = right_t
        left = left_ref[near]
        left = jnp.concatenate([left[0:64], left[64:128]], axis=1)

        def channels(i, acc):
            base = i * CHUNK
            tiles = []
            for q in range(CHUNK):
                w_row = w_bcast_ref[base + q]
                for g in range(4):
                    tiles.append(left[g * 16 : (g + 1) * 16] * w_row)
            act = jnp.dot(
                jnp.concatenate(tiles, axis=0), rhs_ref[...], preferred_element_type=f32
            )
            for q in range(CHUNK):
                floor = floor_ref[pl.ds(base + q, 1), :]
                gate = gate_ref[pl.ds(base + q, 1), :]
                acc = acc + jnp.maximum(act[q * 64 : (q + 1) * 64], floor) * gate
            return acc

        acc = lax.fori_loop(
            0, 2 * chans // CHUNK, channels, jnp.zeros((64, 2 * BLOCK), f32), unroll=2 * chans // CHUNK
        )
        logit_ref[0:64] = acc[:, 0:BLOCK] + offset
        logit_ref[64:128] = acc[:, BLOCK : 2 * BLOCK] + offset
        geo_t_ref[...] = geo_ref[near].T
        valid = valid_tab[slot].astype(f32)
        far = geo_recv_ref[d, j]

        def geometry(i, fape):
            rows = pl.ds(pl.multiple_of(i * 32, 32), 32)
            geo = geo_t_ref[rows, :]
            gaps = [
                far[m : m + 1] - geo[:, 9 + m : 10 + m] for m in range(3)
            ]
            true_gaps = [
                far[3 + m : 4 + m] - geo[:, 21 + m : 22 + m] for m in range(3)
            ]
            dist_sq = jnp.full((32, BLOCK), 0.0001, f32)
            for k in range(3):
                pred = sum(geo[:, 3 * m + k : 3 * m + k + 1] * gaps[m] for m in range(3))
                true = sum(
                    geo[:, 12 + 3 * m + k : 13 + 3 * m + k] * true_gaps[m] for m in range(3)
                )
                dist_sq = dist_sq + (pred - true) ** 2
            clipped = jnp.minimum(jnp.sqrt(dist_sq), 10.0)
            live = geo[:, 24:25] * (far[6:7] * valid)
            live = jnp.where(geo[:, 25:26] != far[7:8], live, 0.0)
            weight = jax.nn.sigmoid(logit_ref[rows, :]) * live
            weight_ref[rows, :] = weight.astype(bf16)
            scored = weight * clipped
            return fape + scored[0:8] + scored[8:16] + scored[16:24] + scored[24:32]

        fape = lax.fori_loop(0, 4, geometry, jnp.zeros((8, BLOCK), f32), unroll=2)
        fape = jnp.sum(jnp.sum(fape, axis=0, keepdims=True), axis=1, keepdims=True)
        fape = fape * (1.0 / (BLOCK * BLOCK))
        fape_own_ref[...] += jnp.where(lane_ids == pos_tab[slot], fape, 0.0)
        weight = weight_ref[...]
        scale = BLOCK ** (-0.5)
        to_second = lax.dot_general(
            weight, value_ref[near], (((0,), (0,)), ((), ())), preferred_element_type=f32
        )
        back_send_ref[d, j] = (to_second * scale).astype(bf16)
        to_first = jnp.dot(
            weight, recv_ref[d, j, :, BLOCK : 2 * BLOCK], preferred_element_type=f32
        )
        first_ref[d, j] = (to_first * scale).astype(bf16)

    def shard_step(d, carry):
        @pl.when(d > 0)
        def _():
            for copy in row_copies(d):
                copy.wait()

        def pair_step(j, inner):
            one_pair(d, j)
            return inner

        lax.fori_loop(0, slots, pair_step, 0)

        @pl.when(d > 0)
        def _():
            back_copy(d).start()

        return carry

    lax.fori_loop(0, res_count, shard_step, 0)

    fape_copy = pltpu.make_async_remote_copy(
        src_ref=fape_own_ref,
        dst_ref=fape_other_ref,
        send_sem=fape_sems.at[0],
        recv_sem=fape_sems.at[1],
        device_id={"ch": 1 - core},
        device_id_type=MESH,
    )
    fape_copy.start()

    row_id = lax.broadcasted_iota(jnp.int32, (blocks * 16, total * 16), 0)
    col_id = lax.broadcasted_iota(jnp.int32, (blocks * 16, total * 16), 1)
    same_row = (row_id % 16) == (col_id % 16)
    row_block = row_id // 16
    col_slot = lax.broadcasted_iota(jnp.int32, (1, total * 16), 1) // 16

    def spread(table):
        chosen = jnp.zeros((1, total * 16), jnp.int32)
        for s in range(total):
            chosen = jnp.where(col_slot == s, table[s], chosen)
        return jnp.where(same_row & (row_block == chosen), 1.0, 0.0).astype(bf16)

    near_hot = spread(near_tab)
    send_hot = spread(send_tab)

    def wait_back(d, carry):
        back_copy(d).wait()
        return carry

    def near_part(g):
        tiles = first_ref[:, :, g * 16 : (g + 1) * 16, :].reshape(total * 16, BLOCK)
        return jnp.dot(near_hot, tiles, preferred_element_type=f32)

    for g in range(BLOCK // 16):
        delta_ref[:, g * 16 : (g + 1) * 16, :] = near_part(g).reshape(blocks, 16, BLOCK)

    lax.fori_loop(1, res_count, wait_back, 0)
    back_recv_ref[0] = back_send_ref[0]
    for g in range(BLOCK // 16):
        tiles = back_recv_ref[:, :, g * 16 : (g + 1) * 16, :].reshape(total * 16, BLOCK)
        part = jnp.dot(send_hot, tiles, preferred_element_type=f32)
        delta_ref[:, g * 16 : (g + 1) * 16, :] += part.reshape(blocks, 16, BLOCK)

    half_send_ref[...] = delta_ref[pl.ds((1 - core) * half, half)].astype(bf16)

    half_copy = pltpu.make_async_remote_copy(
        src_ref=half_send_ref,
        dst_ref=half_recv_ref,
        send_sem=half_sems.at[0],
        recv_sem=half_sems.at[1],
        device_id={"ch": 1 - core},
        device_id_type=MESH,
    )
    half_copy.start()
    half_copy.wait()

    def cross_copy(step, i):
        return pltpu.make_async_remote_copy(
            src_ref=cross_send_ref.at[i],
            dst_ref=cross_recv_ref.at[step, i],
            send_sem=cross_send_sem.at[step, i],
            recv_sem=cross_recv_sem.at[step, i],
            device_id={"blk": lax.rem(blk + step, blk_count)},
            device_id_type=MESH,
        )

    def low_copy(i):
        return pltpu.make_async_remote_copy(
            src_ref=low_own_ref.at[i],
            dst_ref=low_other_ref.at[i],
            send_sem=low_send_sem.at[i],
            recv_sem=low_recv_sem.at[i],
            device_id={"ch": 1 - core},
            device_id_type=MESH,
        )

    def cross_start(i, carry):
        own = delta_ref[pl.ds(core * half + i * piece, piece)]
        own = (own + half_recv_ref[pl.ds(i * piece, piece)].astype(f32)).astype(bf16)
        cross_send_ref[i] = own
        cross_recv_ref[0, i] = own
        for step in range(1, blk_count):
            cross_copy(step, i).start()
        return carry

    lax.fori_loop(0, parts, cross_start, 0)

    def write(low, first_block):
        rows = pl.ds(pl.multiple_of(first_block * BLOCK, BLOCK), piece * BLOCK)
        low = low.reshape(piece * BLOCK, BLOCK)
        grown = jnp.dot(low, w_out_ref[...], preferred_element_type=f32)
        updated_ref[rows, :] = (single_ref[rows, :].astype(f32) + grown).astype(bf16)

    def own_piece(i, carry):
        for step in range(1, blk_count):
            cross_copy(step, i).wait()
        terms = [
            cross_recv_ref[lax.rem(blk - x + blk_count, blk_count), i].astype(f32)
            for x in range(blk_count)
        ]
        low_own_ref[i] = sum(terms[1:], terms[0]).astype(bf16)
        low_copy(i).start()
        write(low_own_ref[i], core * half + i * piece)
        return carry

    lax.fori_loop(0, parts, own_piece, 0)

    fape_copy.wait()
    fape_ref[...] = fape_own_ref[...] + fape_other_ref[...]

    def other_piece(i, carry):
        low_copy(i).wait()
        write(low_other_ref[i], (1 - core) * half + i * piece)
        return carry

    lax.fori_loop(0, parts, other_piece, 0)


def shards(
    single,
    frames,
    teacher,
    res_mask,
    chain_ids,
    block_pairs,
    w_left,
    w_right,
    w_value,
    w_pair,
    pair_bias,
    gate_vec,
    w_out,
):
    res_count = lax.axis_size("res")
    blk_count = lax.axis_size("blk")
    core_count = lax.axis_size("ch")
    row_count, width = single.shape
    blocks = row_count // BLOCK
    pair_dev = block_pairs.shape[1]
    capacity = 1 + (pair_dev + res_count - 2) // res_count
    slots = -(-capacity // core_count)
    chans = w_pair.shape[1]
    parts = 4
    half = blocks // 2
    piece = half // parts
    f32, bf16 = jnp.float32, jnp.bfloat16
    vmem = pl.BlockSpec(memory_space=pltpu.VMEM)
    hbm = pl.BlockSpec(memory_space=pltpu.HBM)
    smem = pl.BlockSpec(memory_space=pltpu.SMEM)
    dma = pltpu.SemaphoreType.DMA
    total = res_count * slots
    sizes = (res_count, blk_count, blocks, pair_dev, slots, chans, parts)
    operands = (
        single,
        frames,
        teacher,
        res_mask[None, :],
        chain_ids[None, :],
        w_left,
        w_right,
        w_value,
        w_pair.T,
        pair_bias[None, :],
        gate_vec[None, :],
        w_out,
    )
    updated, fape = pl.pallas_call(
        functools.partial(pair_kernel, sizes),
        out_shape=(
            jax.ShapeDtypeStruct((row_count, width), bf16),
            jax.ShapeDtypeStruct((8, BLOCK), f32),
        ),
        in_specs=[smem] + [hbm] * len(operands),
        out_specs=(vmem, vmem),
        scratch_shapes=[
            pltpu.VMEM((blocks, BLOCK, BLOCK), bf16),
            pltpu.VMEM((blocks, BLOCK, BLOCK), bf16),
            pltpu.VMEM((blocks, BLOCK, BLOCK), bf16),
            pltpu.VMEM((blocks, 32, BLOCK), f32),
            pltpu.VMEM((blocks, 8, BLOCK), f32),
            pltpu.VMEM((2, 3, chans, BLOCK), f32),
            pltpu.VMEM((2 * chans, 16, 2 * BLOCK), bf16),
            pltpu.VMEM((2 * chans, 2 * BLOCK), f32),
            pltpu.VMEM((2 * chans, 2 * BLOCK), f32),
            pltpu.SMEM((total,), jnp.int32),
            pltpu.SMEM((total,), jnp.int32),
            pltpu.SMEM((total,), jnp.int32),
            pltpu.SMEM((total,), jnp.int32),
            pltpu.VMEM((res_count, slots, BLOCK, 2 * BLOCK), bf16),
            pltpu.VMEM((res_count, slots, BLOCK, 2 * BLOCK), bf16),
            pltpu.VMEM((res_count, slots, 8, BLOCK), f32),
            pltpu.VMEM((res_count, slots, 8, BLOCK), f32),
            pltpu.VMEM((2 * BLOCK, 2 * BLOCK), bf16),
            pltpu.VMEM((BLOCK, BLOCK), f32),
            pltpu.VMEM((BLOCK, 32), f32),
            pltpu.VMEM((BLOCK, BLOCK), bf16),
            pltpu.VMEM((res_count, slots, BLOCK, BLOCK), bf16),
            pltpu.VMEM((res_count, slots, BLOCK, BLOCK), bf16),
            pltpu.VMEM((res_count, slots, BLOCK, BLOCK), bf16),
            pltpu.VMEM((blocks, BLOCK, BLOCK), f32),
            pltpu.VMEM((half, BLOCK, BLOCK), bf16),
            pltpu.VMEM((half, BLOCK, BLOCK), bf16),
            pltpu.VMEM((parts, piece, BLOCK, BLOCK), bf16),
            pltpu.VMEM((blk_count, parts, piece, BLOCK, BLOCK), bf16),
            pltpu.VMEM((parts, piece, BLOCK, BLOCK), bf16),
            pltpu.VMEM((parts, piece, BLOCK, BLOCK), bf16),
            pltpu.VMEM((8, BLOCK), f32),
            pltpu.VMEM((8, BLOCK), f32),
            dma((2,)),
            dma((res_count,)),
            dma((res_count,)),
            dma((res_count,)),
            dma((res_count,)),
            dma((res_count,)),
            dma((res_count,)),
            dma((2,)),
            dma((blk_count, parts)),
            dma((blk_count, parts)),
            dma((parts,)),
            dma((parts,)),
            dma((2,)),
            *[pltpu.VMEM(x.shape, x.dtype) for x in operands],
            dma((len(operands),)),
        ],
        compiler_params=pltpu.CompilerParams(
            collective_id=0, has_side_effects=True, vmem_limit_bytes=63 * 1024 * 1024
        ),
    )(
        block_pairs.reshape(-1),
        *operands,
    )
    return (updated, fape[0, :pair_dev])


def solution(mesh):
    placed = (
        P(("groups", "res"), None),
        P(None, ("groups", "res")),
        P(None, ("groups", "res")),
        P(("groups", "res")),
        P(("groups", "res")),
        P("groups", None, None),
        P(),
        P(),
        P(),
        P(None, "ch"),
        P("ch"),
        P("ch"),
        P(),
    )
    return jax.shard_map(
        shards,
        mesh=mesh,
        in_specs=placed,
        out_specs=(P(("groups", "res"), None), P(("groups", "res", "blk"))),
        check_vma=False,
    )
```

```python
import functools
import jax
import jax.numpy as jnp
from jax import lax
from jax.experimental import pallas as pl
from jax.experimental.pallas import tpu as pltpu
from jax.sharding import PartitionSpec as P

BLOCK = 128
CHUNK = 8
MESH = pl.DeviceIdType.MESH


def pair_kernel(
    sizes,
    pairs_ref,
    *refs,
):
    inputs, refs = refs[:12], refs[12:]
    (
        updated_ref,
        fape_ref,
        left_ref,
        value_ref,
        right_ref,
        geo_ref,
        far_geo_ref,
        pack_ref,
        w_bcast_ref,
        floor_ref,
        gate_ref,
        send_tab,
        near_tab,
        valid_tab,
        pos_tab,
        send_ref,
        recv_ref,
        geo_send_ref,
        geo_recv_ref,
        rhs_ref,
        logit_ref,
        geo_t_ref,
        weight_ref,
        first_ref,
        back_send_ref,
        back_recv_ref,
        delta_ref,
        half_send_ref,
        half_recv_ref,
        cross_send_ref,
        cross_recv_ref,
        low_own_ref,
        low_other_ref,
        fape_own_ref,
        fape_other_ref,
        w_sems,
        row_send_sem,
        row_recv_sem,
        geo_send_sem,
        geo_recv_sem,
        back_send_sem,
        back_recv_sem,
        half_sems,
        cross_send_sem,
        cross_recv_sem,
        low_send_sem,
        low_recv_sem,
        fape_sems,
        single_ref,
        frames_ref,
        teacher_ref,
        mask_ref,
        chain_ref,
        w_left_ref,
        w_right_ref,
        w_value_ref,
        w_pair_ref,
        bias_ref,
        gate_vec_ref,
        w_out_ref,
        load_sems,
    ) = refs
    held = (
        single_ref,
        frames_ref,
        teacher_ref,
        mask_ref,
        chain_ref,
        w_left_ref,
        w_right_ref,
        w_value_ref,
        w_pair_ref,
        bias_ref,
        gate_vec_ref,
        w_out_ref,
    )

    def load(i):
        return pltpu.make_async_copy(inputs[i], held[i], load_sems.at[i])

    for i in (1, 2, 3, 4, 0, 5, 6, 7, 8, 9, 10, 11):
        load(i).start()
    res_count, blk_count, blocks, pair_dev, slots, chans, parts = sizes
    total = res_count * slots
    half = blocks // 2
    piece = half // parts
    res = lax.axis_index("res")
    blk = lax.axis_index("blk")
    core = lax.axis_index("ch")
    f32, bf16 = jnp.float32, jnp.bfloat16

    barrier = pltpu.get_barrier_semaphore()

    def greet(step, carry):
        pl.semaphore_signal(
            barrier,
            inc=1,
            device_id={"res": lax.rem(res + step, res_count)},
            device_id_type=MESH,
        )
        return carry

    lax.fori_loop(1, res_count, greet, 0)
    pl.semaphore_signal(barrier, inc=1, device_id={"ch": 1 - core}, device_id_type=MESH)
    for step in range(1, blk_count):
        pl.semaphore_signal(
            barrier,
            inc=1,
            device_id={"blk": lax.rem(blk + step, blk_count)},
            device_id_type=MESH,
        )

    def lookup(owner, shard):
        base = owner * (pair_dev * 2)
        zero = jnp.int32(0)
        rank = zero
        found = [[zero, zero, zero, zero] for _ in range(slots)]
        for p in range(pair_dev):
            first = pairs_ref[base + 2 * p]
            second = pairs_ref[base + 2 * p + 1]
            hit = (second >= shard * blocks) & (second < (shard + 1) * blocks)
            for j in range(slots):
                match = hit & (rank == 2 * j + core)
                old = found[j]
                found[j] = [
                    jnp.where(match, jnp.clip(first - res * blocks, 0, blocks - 1), old[0]),
                    jnp.where(match, second - shard * blocks, old[1]),
                    jnp.where(match, 1, old[2]),
                    jnp.where(match, p, old[3]),
                ]
            rank = rank + jnp.where(hit, 1, 0)
        return found

    def fill_tables(d, carry):
        out = lookup(lax.rem(res + d, res_count) * blk_count + blk, res)
        own = lookup(res * blk_count + blk, lax.rem(res - d + res_count, res_count))
        for j in range(slots):
            send_tab[d * slots + j] = out[j][1]
            near_tab[d * slots + j] = own[j][0]
            valid_tab[d * slots + j] = own[j][2]
            pos_tab[d * slots + j] = own[j][3]
        return carry

    lax.fori_loop(0, res_count, fill_tables, 0)
    for i in range(12):
        load(i).wait()
    pack_ref[0, 0] = w_pair_ref[...].astype(f32)
    pack_ref[0, 1] = jnp.broadcast_to(-bias_ref[...], (BLOCK, chans)).T
    pack_ref[0, 2] = jnp.broadcast_to(gate_vec_ref[...], (BLOCK, chans)).T

    def features(n, carry):
        rows = single_ref[pl.ds(pl.multiple_of(n * BLOCK, BLOCK), BLOCK), :]
        left_ref[n] = jnp.dot(rows, w_left_ref[...], preferred_element_type=f32).astype(bf16)
        right_ref[n] = jnp.dot(rows, w_right_ref[...], preferred_element_type=f32).astype(bf16)
        value_ref[n] = jnp.dot(rows, w_value_ref[...], preferred_element_type=f32).astype(bf16)
        lanes = pl.ds(pl.multiple_of(n * BLOCK, BLOCK), BLOCK)
        frames = frames_ref[:, lanes]
        teacher = teacher_ref[:, lanes]
        mask = mask_ref[:, lanes].astype(f32)
        chain = chain_ref[:, lanes].astype(f32)
        geo_ref[n] = jnp.concatenate(
            [frames, teacher, mask, chain, jnp.zeros((6, BLOCK), f32)], axis=0
        )
        far_geo_ref[n] = jnp.concatenate([frames[9:12], teacher[9:12], mask, chain], axis=0)
        return carry

    lax.fori_loop(0, blocks, features, 0, unroll=4)

    pl.semaphore_wait(barrier, res_count + blk_count - 1)

    w_copy = pltpu.make_async_remote_copy(
        src_ref=pack_ref.at[0],
        dst_ref=pack_ref.at[1],
        send_sem=w_sems.at[0],
        recv_sem=w_sems.at[1],
        device_id={"ch": 1 - core},
        device_id_type=MESH,
    )
    w_copy.start()

    def row_copies(d):
        target = {"res": lax.rem(res + d, res_count)}
        return (
            pltpu.make_async_remote_copy(
                src_ref=send_ref.at[d],
                dst_ref=recv_ref.at[d],
                send_sem=row_send_sem.at[d],
                recv_sem=row_recv_sem.at[d],
                device_id=target,
                device_id_type=MESH,
            ),
            pltpu.make_async_remote_copy(
                src_ref=geo_send_ref.at[d],
                dst_ref=geo_recv_ref.at[d],
                send_sem=geo_send_sem.at[d],
                recv_sem=geo_recv_sem.at[d],
                device_id=target,
                device_id_type=MESH,
            ),
        )

    def assemble(d, rows_to, geo_to):
        for j in range(slots):
            n = send_tab[d * slots + j]
            rows_to[d, j, :, 0:BLOCK] = right_ref[n]
            rows_to[d, j, :, BLOCK : 2 * BLOCK] = value_ref[n]
            geo_to[d, j] = far_geo_ref[n]

    def send_rows(d, carry):
        assemble(d, send_ref, geo_send_ref)
        for copy in row_copies(d):
            copy.start()
        return carry

    lax.fori_loop(1, res_count, send_rows, 0)
    assemble(0, recv_ref, geo_recv_ref)

    w_copy.wait()
    for h in range(2):
        floor_ref[h * chans : (h + 1) * chans, :] = jnp.concatenate(
            [pack_ref[h, 1]] * 2, axis=1
        )
        gate_ref[h * chans : (h + 1) * chans, :] = jnp.concatenate(
            [pack_ref[h, 2]] * 2, axis=1
        )
        for c in range(chans):
            row = jnp.broadcast_to(pack_ref[h, 0, c : c + 1, :], (16, BLOCK)).astype(bf16)
            w_bcast_ref[h * chans + c] = jnp.concatenate([row, row], axis=1)
    offset = -jnp.sum(floor_ref[:, 0:BLOCK] * gate_ref[:, 0:BLOCK], axis=0, keepdims=True)
    rhs_ref[...] = jnp.zeros_like(rhs_ref)
    fape_own_ref[...] = jnp.zeros_like(fape_own_ref)
    lane_ids = lax.broadcasted_iota(jnp.int32, (8, BLOCK), 1)

    def back_copy(d):
        return pltpu.make_async_remote_copy(
            src_ref=back_send_ref.at[d],
            dst_ref=back_recv_ref.at[d],
            send_sem=back_send_sem.at[d],
            recv_sem=back_recv_sem.at[d],
            device_id={"res": lax.rem(res - d + res_count, res_count)},
            device_id_type=MESH,
        )

    def one_pair(d, j):
        slot = d * slots + j
        near = near_tab[slot]
        right_t = recv_ref[d, j, :, 0:BLOCK].astype(f32).T.astype(bf16)
        rhs_ref[0:BLOCK, 0:BLOCK] = right_t
        rhs_ref[BLOCK : 2 * BLOCK, BLOCK : 2 * BLOCK] = right_t
        left = left_ref[near]
        left = jnp.concatenate([left[0:64], left[64:128]], axis=1)

        def channels(i, acc):
            base = i * CHUNK
            tiles = []
            for q in range(CHUNK):
                w_row = w_bcast_ref[base + q]
                for g in range(4):
                    tiles.append(left[g * 16 : (g + 1) * 16] * w_row)
            act = jnp.dot(
                jnp.concatenate(tiles, axis=0), rhs_ref[...], preferred_element_type=f32
            )
            for q in range(CHUNK):
                floor = floor_ref[pl.ds(base + q, 1), :]
                gate = gate_ref[pl.ds(base + q, 1), :]
                acc = acc + jnp.maximum(act[q * 64 : (q + 1) * 64], floor) * gate
            return acc

        acc = lax.fori_loop(
            0, 2 * chans // CHUNK, channels, jnp.zeros((64, 2 * BLOCK), f32), unroll=2 * chans // CHUNK
        )
        logit_ref[0:64] = acc[:, 0:BLOCK] + offset
        logit_ref[64:128] = acc[:, BLOCK : 2 * BLOCK] + offset
        geo_t_ref[...] = geo_ref[near].T
        valid = valid_tab[slot].astype(f32)
        far = geo_recv_ref[d, j]

        def geometry(i, fape):
            rows = pl.ds(pl.multiple_of(i * 32, 32), 32)
            geo = geo_t_ref[rows, :]
            gaps = [
                far[m : m + 1] - geo[:, 9 + m : 10 + m] for m in range(3)
            ]
            true_gaps = [
                far[3 + m : 4 + m] - geo[:, 21 + m : 22 + m] for m in range(3)
            ]
            dist_sq = jnp.full((32, BLOCK), 0.0001, f32)
            for k in range(3):
                pred = sum(geo[:, 3 * m + k : 3 * m + k + 1] * gaps[m] for m in range(3))
                true = sum(
                    geo[:, 12 + 3 * m + k : 13 + 3 * m + k] * true_gaps[m] for m in range(3)
                )
                dist_sq = dist_sq + (pred - true) ** 2
            clipped = jnp.minimum(jnp.sqrt(dist_sq), 10.0)
            live = geo[:, 24:25] * (far[6:7] * valid)
            live = jnp.where(geo[:, 25:26] != far[7:8], live, 0.0)
            weight = jax.nn.sigmoid(logit_ref[rows, :]) * live
            weight_ref[rows, :] = weight.astype(bf16)
            scored = weight * clipped
            return fape + scored[0:8] + scored[8:16] + scored[16:24] + scored[24:32]

        fape = lax.fori_loop(0, 4, geometry, jnp.zeros((8, BLOCK), f32), unroll=4)
        fape = jnp.sum(jnp.sum(fape, axis=0, keepdims=True), axis=1, keepdims=True)
        fape = fape * (1.0 / (BLOCK * BLOCK))
        fape_own_ref[...] += jnp.where(lane_ids == pos_tab[slot], fape, 0.0)
        weight = weight_ref[...]
        scale = BLOCK ** (-0.5)
        to_second = lax.dot_general(
            weight, value_ref[near], (((0,), (0,)), ((), ())), preferred_element_type=f32
        )
        back_send_ref[d, j] = (to_second * scale).astype(bf16)
        to_first = jnp.dot(
            weight, recv_ref[d, j, :, BLOCK : 2 * BLOCK], preferred_element_type=f32
        )
        first_ref[d, j] = (to_first * scale).astype(bf16)

    def shard_step(d, carry):
        @pl.when(d > 0)
        def _():
            for copy in row_copies(d):
                copy.wait()

        def pair_step(j, inner):
            one_pair(d, j)
            return inner

        lax.fori_loop(0, slots, pair_step, 0)

        @pl.when(d > 0)
        def _():
            back_copy(d).start()

        return carry

    lax.fori_loop(0, res_count, shard_step, 0)

    fape_copy = pltpu.make_async_remote_copy(
        src_ref=fape_own_ref,
        dst_ref=fape_other_ref,
        send_sem=fape_sems.at[0],
        recv_sem=fape_sems.at[1],
        device_id={"ch": 1 - core},
        device_id_type=MESH,
    )
    fape_copy.start()

    row_id = lax.broadcasted_iota(jnp.int32, (blocks * 16, total * 16), 0)
    col_id = lax.broadcasted_iota(jnp.int32, (blocks * 16, total * 16), 1)
    same_row = (row_id % 16) == (col_id % 16)
    row_block = row_id // 16
    col_slot = lax.broadcasted_iota(jnp.int32, (1, total * 16), 1) // 16

    def spread(table):
        chosen = jnp.zeros((1, total * 16), jnp.int32)
        for s in range(total):
            chosen = jnp.where(col_slot == s, table[s], chosen)
        return jnp.where(same_row & (row_block == chosen), 1.0, 0.0).astype(bf16)

    near_hot = spread(near_tab)
    send_hot = spread(send_tab)

    def wait_back(d, carry):
        back_copy(d).wait()
        return carry

    def near_part(g):
        tiles = first_ref[:, :, g * 16 : (g + 1) * 16, :].reshape(total * 16, BLOCK)
        return jnp.dot(near_hot, tiles, preferred_element_type=f32)

    for g in range(BLOCK // 16):
        delta_ref[:, g * 16 : (g + 1) * 16, :] = near_part(g).reshape(blocks, 16, BLOCK)

    lax.fori_loop(1, res_count, wait_back, 0)
    back_recv_ref[0] = back_send_ref[0]
    for g in range(BLOCK // 16):
        tiles = back_recv_ref[:, :, g * 16 : (g + 1) * 16, :].reshape(total * 16, BLOCK)
        part = jnp.dot(send_hot, tiles, preferred_element_type=f32)
        delta_ref[:, g * 16 : (g + 1) * 16, :] += part.reshape(blocks, 16, BLOCK)

    half_send_ref[...] = delta_ref[pl.ds((1 - core) * half, half)].astype(bf16)

    def half_copy(i):
        return pltpu.make_async_remote_copy(
            src_ref=half_send_ref.at[pl.ds(i * piece, piece)],
            dst_ref=half_recv_ref.at[pl.ds(i * piece, piece)],
            send_sem=half_sems.at[0, i],
            recv_sem=half_sems.at[1, i],
            device_id={"ch": 1 - core},
            device_id_type=MESH,
        )

    for i in range(parts):
        half_copy(i).start()

    def cross_copy(step, i):
        return pltpu.make_async_remote_copy(
            src_ref=cross_send_ref.at[i],
            dst_ref=cross_recv_ref.at[step, i],
            send_sem=cross_send_sem.at[step, i],
            recv_sem=cross_recv_sem.at[step, i],
            device_id={"blk": lax.rem(blk + step, blk_count)},
            device_id_type=MESH,
        )

    def low_copy(i):
        return pltpu.make_async_remote_copy(
            src_ref=low_own_ref.at[i],
            dst_ref=low_other_ref.at[i],
            send_sem=low_send_sem.at[i],
            recv_sem=low_recv_sem.at[i],
            device_id={"ch": 1 - core},
            device_id_type=MESH,
        )

    def cross_start(i, carry):
        half_copy(i).wait()
        own = delta_ref[pl.ds(core * half + i * piece, piece)]
        own = (own + half_recv_ref[pl.ds(i * piece, piece)].astype(f32)).astype(bf16)
        cross_send_ref[i] = own
        cross_recv_ref[0, i] = own
        for step in range(1, blk_count):
            cross_copy(step, i).start()
        return carry

    lax.fori_loop(0, parts, cross_start, 0)

    def write(low, first_block):
        rows = pl.ds(pl.multiple_of(first_block * BLOCK, BLOCK), piece * BLOCK)
        low = low.reshape(piece * BLOCK, BLOCK)
        grown = jnp.dot(low, w_out_ref[...], preferred_element_type=f32)
        updated_ref[rows, :] = (single_ref[rows, :].astype(f32) + grown).astype(bf16)

    def own_piece(i, carry):
        for step in range(1, blk_count):
            cross_copy(step, i).wait()
        terms = [
            cross_recv_ref[lax.rem(blk - x + blk_count, blk_count), i].astype(f32)
            for x in range(blk_count)
        ]
        low_own_ref[i] = sum(terms[1:], terms[0]).astype(bf16)
        low_copy(i).start()
        write(low_own_ref[i], core * half + i * piece)
        return carry

    lax.fori_loop(0, parts, own_piece, 0)

    fape_copy.wait()
    fape_ref[...] = fape_own_ref[...] + fape_other_ref[...]

    def other_piece(i, carry):
        low_copy(i).wait()
        write(low_other_ref[i], (1 - core) * half + i * piece)
        return carry

    lax.fori_loop(0, parts, other_piece, 0)


def shards(
    single,
    frames,
    teacher,
    res_mask,
    chain_ids,
    block_pairs,
    w_left,
    w_right,
    w_value,
    w_pair,
    pair_bias,
    gate_vec,
    w_out,
):
    res_count = lax.axis_size("res")
    blk_count = lax.axis_size("blk")
    core_count = lax.axis_size("ch")
    row_count, width = single.shape
    blocks = row_count // BLOCK
    pair_dev = block_pairs.shape[1]
    capacity = 1 + (pair_dev + res_count - 2) // res_count
    slots = -(-capacity // core_count)
    chans = w_pair.shape[1]
    parts = 4
    half = blocks // 2
    piece = half // parts
    f32, bf16 = jnp.float32, jnp.bfloat16
    vmem = pl.BlockSpec(memory_space=pltpu.VMEM)
    hbm = pl.BlockSpec(memory_space=pltpu.HBM)
    smem = pl.BlockSpec(memory_space=pltpu.SMEM)
    dma = pltpu.SemaphoreType.DMA
    total = res_count * slots
    sizes = (res_count, blk_count, blocks, pair_dev, slots, chans, parts)
    operands = (
        single,
        frames,
        teacher,
        res_mask[None, :],
        chain_ids[None, :],
        w_left,
        w_right,
        w_value,
        w_pair.T,
        pair_bias[None, :],
        gate_vec[None, :],
        w_out,
    )
    updated, fape = pl.pallas_call(
        functools.partial(pair_kernel, sizes),
        out_shape=(
            jax.ShapeDtypeStruct((row_count, width), bf16),
            jax.ShapeDtypeStruct((8, BLOCK), f32),
        ),
        in_specs=[smem] + [hbm] * len(operands),
        out_specs=(vmem, vmem),
        scratch_shapes=[
            pltpu.VMEM((blocks, BLOCK, BLOCK), bf16),
            pltpu.VMEM((blocks, BLOCK, BLOCK), bf16),
            pltpu.VMEM((blocks, BLOCK, BLOCK), bf16),
            pltpu.VMEM((blocks, 32, BLOCK), f32),
            pltpu.VMEM((blocks, 8, BLOCK), f32),
            pltpu.VMEM((2, 3, chans, BLOCK), f32),
            pltpu.VMEM((2 * chans, 16, 2 * BLOCK), bf16),
            pltpu.VMEM((2 * chans, 2 * BLOCK), f32),
            pltpu.VMEM((2 * chans, 2 * BLOCK), f32),
            pltpu.SMEM((total,), jnp.int32),
            pltpu.SMEM((total,), jnp.int32),
            pltpu.SMEM((total,), jnp.int32),
            pltpu.SMEM((total,), jnp.int32),
            pltpu.VMEM((res_count, slots, BLOCK, 2 * BLOCK), bf16),
            pltpu.VMEM((res_count, slots, BLOCK, 2 * BLOCK), bf16),
            pltpu.VMEM((res_count, slots, 8, BLOCK), f32),
            pltpu.VMEM((res_count, slots, 8, BLOCK), f32),
            pltpu.VMEM((2 * BLOCK, 2 * BLOCK), bf16),
            pltpu.VMEM((BLOCK, BLOCK), f32),
            pltpu.VMEM((BLOCK, 32), f32),
            pltpu.VMEM((BLOCK, BLOCK), bf16),
            pltpu.VMEM((res_count, slots, BLOCK, BLOCK), bf16),
            pltpu.VMEM((res_count, slots, BLOCK, BLOCK), bf16),
            pltpu.VMEM((res_count, slots, BLOCK, BLOCK), bf16),
            pltpu.VMEM((blocks, BLOCK, BLOCK), f32),
            pltpu.VMEM((half, BLOCK, BLOCK), bf16),
            pltpu.VMEM((half, BLOCK, BLOCK), bf16),
            pltpu.VMEM((parts, piece, BLOCK, BLOCK), bf16),
            pltpu.VMEM((blk_count, parts, piece, BLOCK, BLOCK), bf16),
            pltpu.VMEM((parts, piece, BLOCK, BLOCK), bf16),
            pltpu.VMEM((parts, piece, BLOCK, BLOCK), bf16),
            pltpu.VMEM((8, BLOCK), f32),
            pltpu.VMEM((8, BLOCK), f32),
            dma((2,)),
            dma((res_count,)),
            dma((res_count,)),
            dma((res_count,)),
            dma((res_count,)),
            dma((res_count,)),
            dma((res_count,)),
            dma((2, parts)),
            dma((blk_count, parts)),
            dma((blk_count, parts)),
            dma((parts,)),
            dma((parts,)),
            dma((2,)),
            *[pltpu.VMEM(x.shape, x.dtype) for x in operands],
            dma((len(operands),)),
        ],
        compiler_params=pltpu.CompilerParams(
            collective_id=0, has_side_effects=True, vmem_limit_bytes=63 * 1024 * 1024
        ),
    )(
        block_pairs.reshape(-1),
        *operands,
    )
    return (updated, fape[0, :pair_dev])


def solution(mesh):
    placed = (
        P(("groups", "res"), None),
        P(None, ("groups", "res")),
        P(None, ("groups", "res")),
        P(("groups", "res")),
        P(("groups", "res")),
        P("groups", None, None),
        P(),
        P(),
        P(),
        P(None, "ch"),
        P("ch"),
        P("ch"),
        P(),
    )
    return jax.shard_map(
        shards,
        mesh=mesh,
        in_specs=placed,
        out_specs=(P(("groups", "res"), None), P(("groups", "res", "blk"))),
        check_vma=False,
    )
```
